512 devices in a mesh: row: 32 (over y, x), col: 16 (over z, core).
Axes of the slice: x: 4, y: 8, z: 8, core: 2. Of those that a mesh axis runs over, the one named last changes fastest.
Arguments:
- top_inverse: float32 [8192, 8192], P('row', 'col'), may hold values from -8 to 8, as said below
- coupling: float32 [2, 8192, 4096], P(None, 'col', 'row'), may hold values from -0.0625 to 0.0625
- child_inverse: float32 [2, 4096, 1024], P(None, 'row'), may hold values from -2 to 2, as said below
- tile_mask: int32 [2, 32], P(None, 'col'), may hold values 0 or 1
Outputs:
- cross_block: float32 [1024, 2, 8192], P('col', None, 'row')
- child_block: float32 [1024, 2, 1024], P('row', None, 'col')
The draws below stay inside these ranges and needn't reach their ends.
Inputs may be any that keep to these rules, and one draw needn't show every extreme that they name: top_inverse is symmetric. `child_inverse`: each child's block is zero above its diagonal: entry (k, i, j) is 0 where i < j. `tile_mask`: the pattern applied to the coupling block per tile of 256 top-separator rows.
All inputs are finite; a program needn't handle non-finite values.
Results may differ from the reference program's by a relative error of at most 0.00011.
Values sent between devices are 32-bit elements; how exact they have to be, the bound alone decides.
A program may use at most 64 MiB of HBM per device.

```python
import jax
import jax.numpy as jnp
from jax import lax

SEP = 8192
CHILD = 4096
CHILDREN = 2
PANEL = 1024
TILE = 256


def draw_top_inverse(key, part):
    key = jax.random.fold_in(key, 11)
    base = jnp.clip(jax.random.normal(key, (SEP, SEP), jnp.float32), -4.0, 4.0)
    symmetric = 0.7 * (base + base.T)
    result = symmetric + 2.0 * jnp.eye(SEP, dtype=jnp.float32)
    return jnp.clip(result, -8.0, 8.0)


def draw_child_inverse(key, part):
    key = jax.random.fold_in(key, 23)
    shape = (CHILDREN, CHILD, PANEL)
    offdiag = jnp.clip(jax.random.normal(key, shape, jnp.float32), -6.0, 6.0) / jnp.sqrt(jnp.float32(CHILD))
    diagonal = jax.random.uniform(jax.random.fold_in(key, 1), shape, jnp.float32, 0.5, 1.5)
    row_index = lax.broadcasted_iota(jnp.int32, shape, 1)
    col_index = lax.broadcasted_iota(jnp.int32, shape, 2)
    below = jnp.where(row_index > col_index, offdiag, 0.0)
    return jnp.where(row_index == col_index, diagonal, below)


def touch_ends(values, stream_key, low, top_value):
    index_at = [jax.random.randint(jax.random.fold_in(stream_key, axis), (), 0, length) for axis, length in enumerate(values.shape)]
    longest = values.shape.index(max(values.shape))
    beside = index_at[:longest] + [(index_at[longest] + 1) % values.shape[longest]] + index_at[longest + 1:]
    return values.at[tuple(index_at)].set(low).at[tuple(beside)].set(top_value)


def block_scale(rng, dims, cuts, least, top_value):
    def one(axis_at, shards_of):
        draws = jax.random.uniform(jax.random.fold_in(jax.random.fold_in(rng, 6), axis_at), (shards_of,), jnp.float32, least / len(cuts), top_value / len(cuts))
        return jnp.repeat(jnp.exp(draws), dims[axis_at] // shards_of).reshape((-1,) + (1,) * (len(dims) - axis_at - 1))

    level = one(*cuts[0])
    for cut in cuts[1:]:
        level = level * one(*cut)
    return level


def noise(stream_key, shape, scale, most, shards=(), held_as=jnp.bfloat16):
    gain = block_scale(stream_key, shape, shards, -0.22, 0.18) if shards else 1.0
    array = jax.random.normal(stream_key, shape, jnp.float32) * scale * gain
    return jnp.minimum(jnp.maximum(array, -most), most).astype(held_as)


def setup_inputs(seed: int = 0) -> dict:
    key_list = jax.random.split(jax.random.key(seed), 5)
    return {
        "top_inverse": draw_top_inverse(jax.random.fold_in(key_list[4], 71), 0),
        "coupling": noise(key_list[1], (CHILDREN, SEP, CHILD), SEP ** -0.5, 0.0625, ((1, 16), (2, 32)), jnp.float32),
        "child_inverse": draw_child_inverse(jax.random.fold_in(key_list[4], 71), 0),
        "tile_mask": touch_ends((jax.random.randint(key_list[3], (CHILDREN, SEP // TILE), 0, 4) < 3).astype(jnp.int32), jax.random.fold_in(key_list[3], 1), 0, 1),
    }


def reference(top_inverse, coupling, child_inverse, tile_mask):
    highest = lax.Precision.HIGHEST
    lower_parts = []
    diag_parts = []
    for member in range(CHILDREN):
        mask_rows = jnp.repeat(tile_mask[member].astype(jnp.float32), TILE)
        masked = coupling[member] * mask_rows[:, None]
        factor = jnp.dot(masked, child_inverse[member], precision=highest, preferred_element_type=jnp.float32)
        image = jnp.dot(top_inverse, factor, precision=highest, preferred_element_type=jnp.float32)
        gram = jnp.dot(child_inverse[member].T, child_inverse[member], precision=highest, preferred_element_type=jnp.float32)
        cross = jnp.dot(factor.T, image, precision=highest, preferred_element_type=jnp.float32)
        lower_parts.append(-image.T)
        diag_parts.append(gram + cross)
    return jnp.stack(lower_parts, axis=1), jnp.stack(diag_parts, axis=1)
```

```python
import jax
import jax.numpy as jnp
from jax import lax
from jax.experimental import pallas as pl
from jax.experimental.pallas import tpu as pltpu
from jax.sharding import PartitionSpec as P

NX, NY, NZ = 4, 8, 8
MESH = pl.DeviceIdType.MESH
F32, BF16 = jnp.float32, jnp.bfloat16
NSEM = 160
EVEN = (4, 2, 6, 0)
ODD = (3, 5, 1, 7)


def split(value):
    high = value.astype(BF16)
    return high, (value - high.astype(F32)).astype(BF16)


def dot_nt(a, b):
    return lax.dot_general(a, b, (((1,), (1,)), ((), ())), preferred_element_type=F32)


def dot3(a_high, a_low, b_high, b_low):
    rows = a_high.shape[0]
    both = dot_nt(jnp.concatenate([a_high, a_low], axis=0), b_high)
    return both[:rows] + both[rows:] + dot_nt(a_high, b_low)


def kernel(
    top_ref, coupling_ref, inverse_ref, mask_ref, cross_ref, child_ref,
    xt, masked, xr, xz, cr, xth, xtl, tr, th, tl, pb, rb, fg, fy, fyh, fyl,
    acc, rd, img, neg, outr, ec, er, ch, chr_, gram, send_sem, recv_sem, last_sem,
):
    row, col = lax.axis_index("row"), lax.axis_index("col")
    x, y = lax.rem(row, NX), lax.div(row, NX)
    h, z = lax.rem(col, 2), lax.div(col, 2)
    k, half = lax.div(x, 2), lax.rem(x, 2)
    other = 1 - h
    parity = lax.rem(y + h, 2)
    own = 2 * h + half

    def at(px, py, pz, ph):
        return (py * NX + px, pz * 2 + ph)

    def xs(d):
        return lax.rem(x + d, NX)

    def ys(d):
        return lax.rem(y + d, NY)

    def zs(d):
        return lax.rem(z + d, NZ)

    started = []
    count = [0]

    def copy(src, dst, device, keep=True):
        i = count[0]
        count[0] += 1
        made = pltpu.make_async_remote_copy(
            src_ref=src, dst_ref=dst, send_sem=send_sem.at[i], recv_sem=recv_sem.at[i],
            device_id=device, device_id_type=MESH,
        )
        if keep:
            started.append(made)
        return made

    barrier = pltpu.get_barrier_semaphore()

    def greet(device):
        pl.semaphore_signal(barrier, inc=1, device_id=device, device_id_type=MESH)

    for d in range(1, NX):
        greet(at(xs(d), y, z, h))
        greet(at(xs(d), y, z, other))
    greet(at(x, y, z, other))
    for d in range(1, NY):
        greet(at(x, ys(d), z, h))
    greet(at(x, y, zs(1), h))
    greet(at(x, y, zs(7), h))

    @pl.when(y != z)
    def _():
        greet(at(x, z, y, h))

    for child in range(2):
        for s in range(8):
            xt[child, s] = inverse_ref[child, :, 128 * s : 128 * s + 128].T

    @pl.when(y != z)
    def _():
        pl.semaphore_wait(barrier, 17)

    @pl.when(y == z)
    def _():
        pl.semaphore_wait(barrier, 16)

    def x_rows(to_half, p):
        return pl.ds(pl.multiple_of(64 * h + 32 * to_half + 16 * p, 16), 16)

    x_copies = []
    for d in (1, 3, 2):
        to = xs(d)
        for p in range(2):
            made = copy(
                xt.at[lax.div(to, 2), :, x_rows(lax.rem(to, 2), p), :], xr.at[x, p], at(to, y, z, h)
            )
            made.start()
            x_copies.append(made)

    for child in range(2):
        for tile in range(2):
            number = mask_ref[child, tile].astype(F32)
            masked[child, 256 * tile : 256 * tile + 256] = (
                coupling_ref[child, 256 * tile : 256 * tile + 256] * number
            )

    def chunk_rows(s):
        dist = EVEN[s] + parity * (ODD[s] - EVEN[s])
        sub = lax.div(ys(dist), 2)
        return pl.ds(pl.multiple_of(128 * sub, 128), 128)

    c_copies = []
    for s in range(4):
        group = []
        for d in (1, 3, 2):
            to = xs(d)
            made = copy(
                masked.at[lax.div(to, 2), chunk_rows(s), :], cr.at[parity, s, x], at(to, y, z, h)
            )
            made.start()
            group.append(made)
        c_copies.append(group)
        cr[parity, s, x] = masked[k, chunk_rows(s), :]
    forwards = [
        copy(cr.at[parity, s], cr.at[parity, s], at(x, y, z, other)) for s in range(4)
    ]

    z_copies = []
    for d in (1, 3, 2):
        to = xs(d)
        made = copy(xt.at[lax.div(to, 2), z], xz.at[x], at(to, y, z, h))
        made.start()
        z_copies.append(made)
    xz[x] = xt[k, z]

    t_copies = []
    for d in (1, 3, 2):
        made = copy(top_ref, tr.at[h, x], at(xs(d), y, z, h))
        made.start()
        t_copies.append((d, made))
    t_forwards = [copy(top_ref, tr.at[h, x], at(x, y, z, other))]
    t_forwards[0].start()
    tr[h, x] = top_ref[...]

    for p in range(2):
        xr[x, p] = xt[k, :, x_rows(half, p), :]
    for made in x_copies:
        made.wait_recv()
    for p in range(2):
        for src in range(4):
            high, low = split(xr[src, p].reshape(128, 128))
            xth[128 * p : 128 * p + 128, 128 * src : 128 * src + 128] = high
            xtl[128 * p : 128 * p + 128, 128 * src : 128 * src + 128] = low

    def partial(which, s):
        @pl.when(parity == which)
        def _():
            for made in c_copies[s]:
                made.wait_recv()
            forwards[s].start()

        @pl.when(parity != which)
        def _():
            forwards[s].wait_recv()

        rows = jnp.concatenate([cr[which, s, src] for src in range(4)], axis=1)
        high, low = split(rows)
        return dot3(xth[...], xtl[...], high, low)

    up, down = at(x, ys(1), z, h), at(x, ys(7), z, h)
    pb[4] = partial(0, 0)
    prev_up = copy(pb.at[4, pl.ds(0, 128)], rb.at[0, 0, pl.ds(0, 128)], up)
    prev_down = copy(pb.at[4, pl.ds(128, 128)], rb.at[1, 0, pl.ds(128, 128)], down)
    prev_up.start()
    prev_down.start()
    pb[3] = partial(1, 0)
    pb[5] = partial(1, 1)
    for step in range(1, 4):
        prev_up.wait_recv()
        if step == 1:
            pb[3, :128] += rb[0, 0, :128]
        else:
            pb[4 - step] += rb[0, step - 1]
        prev_up = copy(pb.at[4 - step], rb.at[0, step], up)
        prev_up.start()
        prev_down.wait_recv()
        if step == 1:
            pb[5, 128:] += rb[1, 0, 128:]
        else:
            pb[4 + step] += rb[1, step - 1]
        prev_down = copy(pb.at[4 + step], rb.at[1, step], down)
        prev_down.start()
        if step == 1:
            pb[2] = partial(0, 1)
            pb[6] = partial(0, 2)
        if step == 2:
            pb[1] = partial(1, 2)
            pb[7] = partial(1, 3)
    pb[0] = partial(0, 3)

    for made in z_copies:
        made.wait_recv()
    high, low = split(jnp.concatenate([xz[src] for src in range(4)], axis=1))
    gram[...] = dot3(xth[...], xtl[...], high, low)

    prev_up.wait_recv()
    prev_down.wait_recv()
    fg[y] = (pb[0] + rb[0, 3] + rb[1, 3]).reshape(2, 128, 128)

    def ring_send(step, p):
        made = []
        for way, peer in ((0, up), (1, down)):
            index = ys(8 - step) if way == 0 else ys(step)
            if step < 3:
                ref = fg.at[index, p]
            else:
                ref = fg.at[index, p, pl.ds(64 * way, 64)]
            made.append(copy(ref, ref, peer))
            made[-1].start()
        return made

    ring = [ring_send(0, p) for p in range(2)]

    flip = copy(fg.at[y], fy.at[y], at(x, z, y, h), keep=False)

    @pl.when(y != z)
    def _():
        flip.start()

    @pl.when(y == z)
    def _():
        fy[z] = fg[y]

    def top_block(index):
        return lax.rem(index, 2), pl.ds(pl.multiple_of(128 * lax.div(index, 2), 128), 128)

    for step in range(1, 4):
        for p in range(2):
            for made in ring[p]:
                made.wait_recv()
            ring[p] = ring_send(step, p)
        d, made = t_copies[step - 1]
        made.wait_recv()
        ref = tr.at[h, xs(4 - d)]
        t_forwards.append(copy(ref, ref, at(x, y, z, other)))
        t_forwards[-1].start()
    for made in t_forwards:
        made.wait_recv()
    pairs = ((0, 4), (1, 7), (2, 6), (3, 5))
    for n, pair in enumerate(pairs):
        for side in range(2):
            core, lanes = top_block(ys(pair[side]))
            for src in range(4):
                high, low = split(tr[core, src, :, lanes])
                th[n, 256 * src : 256 * src + 256, 128 * side : 128 * side + 128] = high
                tl[n, 256 * src : 256 * src + 256, 128 * side : 128 * side + 128] = low

    front, back = at(x, y, zs(1), h), at(x, y, zs(7), h)

    def second_send(step):
        made = []
        for way, peer in ((0, front), (1, back)):
            index = zs(8 - step) if way == 0 else zs(step)
            ref = fy.at[index] if step < 3 else fy.at[index, way]
            made.append(copy(ref, ref, peer))
            made[-1].start()
        return made

    def image_part(p):
        for made in ring[p]:
            made.wait_recv()
        highs, lows = [], []
        for a, b in pairs:
            high, low = split(jnp.concatenate([fg[ys(a), p], fg[ys(b), p]], axis=1))
            highs.append(jnp.concatenate([high, low], axis=0))
            lows.append(high)
        for n in range(4):
            lanes = slice(256 * n, 256 * n + 256)
            total = None
            for i in range(4):
                both = dot_nt(highs[i], th[i, lanes, :])
                part = both[:128] + both[128:] + dot_nt(lows[i], tl[i, lanes, :])
                total = part if total is None else total + part
            acc[p, :, :, lanes] = total.reshape(8, 16, 256)

    def image_first(p):
        made = []
        for way, peer in ((0, front), (1, back)):
            made.append(
                copy(acc.at[p, zs(4), pl.ds(8 * way, 8)], rd.at[p, way, 0, pl.ds(8 * way, 8)], peer)
            )
            made[-1].start()
        return made

    def image_step(p, step, before):
        made = []
        for way, peer in ((0, front), (1, back)):
            before[way].wait_recv()
            index = zs(4 - step) if way == 0 else zs(4 + step)
            if step == 1:
                rows = pl.ds(8 * way, 8)
                acc[p, index, rows] += rd[p, way, 0, rows]
            else:
                acc[p, index] += rd[p, way, step - 1]
            made.append(copy(acc.at[p, index], rd.at[p, way, step], peer))
            made[-1].start()
        return made

    image_part(0)
    moving = [image_first(0), None]
    image_part(1)
    moving[1] = image_first(1)

    @pl.when(y != z)
    def _():
        flip.wait_recv()

    second = second_send(0)
    for step in range(1, 4):
        for p in range(2):
            moving[p] = image_step(p, step, moving[p])
        for made in second:
            made.wait_recv()
        second = second_send(step)

    image_copies, out_copies = [], []
    for p in range(2):
        for made in moving[p]:
            made.wait_recv()
        total = acc[p, z] + rd[p, 0, 3] + rd[p, 1, 3]
        img[own, p] = total
        neg[p] = -total
        for px, ph in ((lax.rem(x + 1 - 2 * half + NX, NX), h), (lax.rem(x + 1 - 2 * half + NX, NX), other), (x, other)):
            made = copy(img.at[own, p], img.at[own, p], at(px, y, z, ph))
            made.start()
            image_copies.append(made)
    for p in range(2):
        for d in (1, 3, 2):
            to = xs(d)
            lanes = pl.ds(pl.multiple_of(256 * to, 256), 256)
            made = copy(neg.at[p, :, lanes], outr.at[x, p], at(to, y, z, h))
            made.start()
            out_copies.append(made)
        outr[x, p] = neg[p, :, pl.ds(pl.multiple_of(256 * x, 256), 256)]

    for made in second:
        made.wait_recv()
    for c in range(8):
        block = 4 * (c % 2) + c // 2
        high, low = split(fy[c].reshape(256, 128))
        fyh[:, 128 * block : 128 * block + 128] = high
        fyl[:, 128 * block : 128 * block + 128] = low

    for made in image_copies:
        made.wait_recv()
    high, low = split(img[...].reshape(128, 1024))
    ec[...] = (gram[...] + dot3(fyh[...], fyl[...], high, low)).reshape(2, 8, 16, 128)
    e_copies = []
    for d in range(1, NY):
        made = copy(ec.at[:, ys(d)], er.at[d - 1], at(x, ys(d), z, h))
        made.start()
        e_copies.append(made)

    for made in out_copies:
        made.wait_recv()
    for src in range(4):
        for p in range(2):
            start = 32 * (src % 2) + 16 * p
            cross_ref[src // 2, start : start + 16] = outr[src, p]

    total = ec[:, y]
    for d in range(1, NY):
        e_copies[d - 1].wait_recv()
        total = total + er[d - 1]
    ch[...] = total.reshape(32, 128)

    def last(ph, sem):
        return pltpu.make_async_remote_copy(
            src_ref=ch, dst_ref=chr_.at[k], send_sem=last_sem.at[2 + sem], recv_sem=last_sem.at[k],
            device_id=at(own, y, z, ph), device_id_type=MESH,
        )

    last(other, 0).start()

    @pl.when(h != k)
    def _():
        last(h, 1).start()

    @pl.when(h == k)
    def _():
        chr_[k] = ch[...]

    def arrived(child):
        pltpu.make_async_remote_copy(
            src_ref=ch, dst_ref=chr_.at[child], send_sem=last_sem.at[2], recv_sem=last_sem.at[child],
            device_id=at(own, y, z, other), device_id_type=MESH,
        ).wait_recv()

    for child in range(2):
        @pl.when(jnp.logical_or(h != k, k != child))
        def _():
            arrived(child)

    @pl.when(h == 0)
    def _():
        child_ref[...] = chr_[:, :, :64]

    @pl.when(h == 1)
    def _():
        child_ref[...] = chr_[:, :, 64:]

    last(other, 0).wait_send()

    @pl.when(h != k)
    def _():
        last(h, 1).wait_send()

    @pl.when(y != z)
    def _():
        flip.wait_send()

    for made in started:
        made.wait_send()


def local(top_inverse, coupling, child_inverse, tile_mask):
    vmem = pl.BlockSpec(memory_space=pltpu.VMEM)
    scratch = [
        pltpu.VMEM((2, 8, 128, 128), F32),
        pltpu.VMEM((2, 512, 128), F32),
        pltpu.VMEM((4, 2, 8, 16, 128), F32),
        pltpu.VMEM((4, 128, 128), F32),
        pltpu.VMEM((2, 4, 4, 128, 128), F32),
        pltpu.VMEM((256, 512), BF16),
        pltpu.VMEM((256, 512), BF16),
        pltpu.VMEM((2, 4, 256, 512), F32),
        pltpu.VMEM((4, 1024, 256), BF16),
        pltpu.VMEM((4, 1024, 256), BF16),
        pltpu.VMEM((8, 256, 128), F32),
        pltpu.VMEM((2, 4, 256, 128), F32),
        pltpu.VMEM((8, 2, 128, 128), F32),
        pltpu.VMEM((8, 2, 128, 128), F32),
        pltpu.VMEM((256, 1024), BF16),
        pltpu.VMEM((256, 1024), BF16),
        pltpu.VMEM((2, 8, 16, 1024), F32),
        pltpu.VMEM((2, 2, 4, 16, 1024), F32),
        pltpu.VMEM((4, 2, 16, 1024), F32),
        pltpu.VMEM((2, 16, 1024), F32),
        pltpu.VMEM((4, 2, 16, 256), F32),
        pltpu.VMEM((2, 8, 16, 128), F32),
        pltpu.VMEM((7, 2, 16, 128), F32),
        pltpu.VMEM((32, 128), F32),
        pltpu.VMEM((2, 32, 128), F32),
        pltpu.VMEM((256, 128), F32),
        pltpu.SemaphoreType.DMA((NSEM,)),
        pltpu.SemaphoreType.DMA((NSEM,)),
        pltpu.SemaphoreType.DMA((4,)),
    ]
    cross, child = pl.pallas_call(
        kernel,
        out_shape=(
            jax.ShapeDtypeStruct((2, 64, 256), F32),
            jax.ShapeDtypeStruct((2, 32, 64), F32),
        ),
        in_specs=[vmem, vmem, vmem, pl.BlockSpec(memory_space=pltpu.SMEM)],
        out_specs=(vmem, vmem),
        scratch_shapes=scratch,
        compiler_params=pltpu.CompilerParams(
            collective_id=0, has_side_effects=True, vmem_limit_bytes=48 << 20
        ),
        name="selected_inverse",
    )(top_inverse, coupling, child_inverse, tile_mask)
    return jnp.transpose(cross, (1, 0, 2)), jnp.transpose(child, (1, 0, 2))


def solution(mesh):
    in_specs = (P("row", "col"), P(None, "col", "row"), P(None, "row", None), P(None, "col"))
    out_specs = (P("col", None, "row"), P("row", None, "col"))
    return jax.shard_map(local, mesh=mesh, in_specs=in_specs, out_specs=out_specs, check_vma=False)
```

```python
import jax
import jax.numpy as jnp
from jax import lax
from jax.experimental import pallas as pl
from jax.experimental.pallas import tpu as pltpu
from jax.sharding import PartitionSpec as P

NX, NY, NZ = 4, 8, 8
MESH = pl.DeviceIdType.MESH
F32, BF16 = jnp.float32, jnp.bfloat16
NSEM = 160
EVEN = (4, 2, 6, 0)
ODD = (3, 5, 1, 7)


def split(value):
    high = value.astype(BF16)
    return high, (value - high.astype(F32)).astype(BF16)


def dot_nt(a, b):
    return lax.dot_general(a, b, (((1,), (1,)), ((), ())), preferred_element_type=F32)


def dot3(a_high, a_low, b_high, b_low):
    rows = a_high.shape[0]
    both = dot_nt(jnp.concatenate([a_high, a_low], axis=0), b_high)
    return both[:rows] + both[rows:] + dot_nt(a_high, b_low)


def kernel(
    top_ref, coupling_ref, inverse_ref, mask_ref, cross_ref, child_ref,
    xin, xt, masked, xr, xz, cr, xb, tr, th, tl, pb, rb, fg, fy, fyh, fyl,
    acc, rd, img, neg, outr, ec, er, ch, chr_, gram, send_sem, recv_sem, last_sem, load_sem,
):
    row, col = lax.axis_index("row"), lax.axis_index("col")
    x, y = lax.rem(row, NX), lax.div(row, NX)
    h, z = lax.rem(col, 2), lax.div(col, 2)
    k, half = lax.div(x, 2), lax.rem(x, 2)
    other = 1 - h
    parity = lax.rem(y + h, 2)
    own = 2 * h + half

    def at(px, py, pz, ph):
        return (py * NX + px, pz * 2 + ph)

    def xs(d):
        return lax.rem(x + d, NX)

    def ys(d):
        return lax.rem(y + d, NY)

    def zs(d):
        return lax.rem(z + d, NZ)

    started = []
    count = [0]

    def copy(src, dst, device, keep=True):
        i = count[0]
        count[0] += 1
        made = pltpu.make_async_remote_copy(
            src_ref=src, dst_ref=dst, send_sem=send_sem.at[i], recv_sem=recv_sem.at[i],
            device_id=device, device_id_type=MESH,
        )
        if keep:
            started.append(made)
        return made

    loads = [
        pltpu.make_async_copy(inverse_ref, xin, load_sem.at[0]),
        pltpu.make_async_copy(coupling_ref, masked, load_sem.at[1]),
        pltpu.make_async_copy(top_ref, tr.at[h, x], load_sem.at[2]),
    ]
    for made in loads:
        made.start()
    barrier = pltpu.get_barrier_semaphore()

    def greet(device):
        pl.semaphore_signal(barrier, inc=1, device_id=device, device_id_type=MESH)

    for d in range(1, NX):
        greet(at(xs(d), y, z, h))
        greet(at(xs(d), y, z, other))
    greet(at(x, y, z, other))
    for d in range(1, NY):
        greet(at(x, ys(d), z, h))
    for d in (1, 2, 6, 7):
        greet(at(x, y, zs(d), h))

    @pl.when(y != z)
    def _():
        greet(at(x, z, y, h))

    loads[0].wait()
    for child in range(2):
        for s in range(8):
            xt[child, s] = xin[child, :, 128 * s : 128 * s + 128].T
    loads[1].wait()
    for child in range(2):
        for tile in range(2):
            number = mask_ref[child, tile].astype(F32)
            masked[child, 256 * tile : 256 * tile + 256] *= number

    @pl.when(y != z)
    def _():
        pl.semaphore_wait(barrier, 19)

    @pl.when(y == z)
    def _():
        pl.semaphore_wait(barrier, 18)

    def x_rows(to_half, p):
        return pl.ds(pl.multiple_of(64 * h + 32 * to_half + 16 * p, 16), 16)

    def x_send(p):
        made = []
        for d in (1, 3, 2):
            to = xs(d)
            made.append(
                copy(
                    xt.at[lax.div(to, 2), :, x_rows(lax.rem(to, 2), p), :],
                    xr.at[x, p],
                    at(to, y, z, h),
                )
            )
            made[-1].start()
        xr[x, p] = xt[k, :, x_rows(half, p), :]
        return made

    def chunk_rows(s):
        dist = EVEN[s] + parity * (ODD[s] - EVEN[s])
        sub = lax.div(ys(dist), 2)
        return pl.ds(pl.multiple_of(128 * sub, 128), 128)

    def c_send(s):
        made = []
        for d in (1, 3, 2):
            to = xs(d)
            made.append(
                copy(
                    masked.at[lax.div(to, 2), chunk_rows(s), :],
                    cr.at[parity, s, x],
                    at(to, y, z, h),
                )
            )
            made[-1].start()
        cr[parity, s, x] = masked[k, chunk_rows(s), :]
        return made

    x_copies = [x_send(0)]
    c_copies = [c_send(0)]
    x_copies.append(x_send(1))
    for s in range(1, 4):
        c_copies.append(c_send(s))
    forwards = [copy(cr.at[parity, s], cr.at[parity, s], at(x, y, z, other)) for s in range(4)]

    loads[2].wait()
    mine = tr.at[h, x]
    t_near = [copy(mine, mine, at(xs(d), y, z, h)) for d in (1, 3)]
    for made in t_near:
        made.start()
    t_cores = [copy(mine, mine, at(x, y, z, other))]
    t_cores[0].start()

    z_copies = []
    for d in (1, 3, 2):
        to = xs(d)
        made = copy(xt.at[lax.div(to, 2), z], xz.at[x], at(to, y, z, h))
        made.start()
        z_copies.append(made)
    xz[x] = xt[k, z]

    def convert(which, src):
        core = lax.rem(y + which, 2)
        rows = pl.ds(pl.multiple_of(256 * src, 256), 256)
        for i in range(2):
            n = which + 2 * i
            for side in range(2):
                far = lax.rem(8 - n, 8) if side else n
                dist = jnp.where(n == 0, 4 * side, far)
                lanes = pl.ds(pl.multiple_of(128 * lax.div(ys(dist), 2), 128), 128)
                high, low = split(tr[core, src, :, lanes])
                th[n, rows, 128 * side : 128 * side + 128] = high
                tl[n, rows, 128 * side : 128 * side + 128] = low

    def x_take(p):
        for made in x_copies[p]:
            made.wait_recv()
        for src in range(4):
            high, low = split(xr[src, p].reshape(128, 128))
            lanes = slice(128 * src, 128 * src + 128)
            xb[p, :128, lanes] = high
            xb[p, 128:, lanes] = low

    def take(which, s):
        @pl.when(parity == which)
        def _():
            for made in c_copies[s]:
                made.wait_recv()
            forwards[s].start()

        @pl.when(parity != which)
        def _():
            forwards[s].wait_recv()

        return split(jnp.concatenate([cr[which, s, src] for src in range(4)], axis=1))

    def partial(rows, p):
        high, low = rows
        both = dot_nt(xb[p], high)
        return both[:128] + both[128:] + dot_nt(xb[p, :128], low)

    def y_at(d):
        return at(x, ys(d), z, h)

    def sent(src, dst, device):
        made = copy(src, dst, device)
        made.start()
        return made

    near = (1, 7)
    over = (2, 6)
    x_take(0)
    rows4 = take(0, 0)
    first = [[None, None], [None, None]]
    moving = [[None, None], [None, None]]

    def far_factor(p):
        pb[4, p] = partial(rows4, p)
        for way in range(2):
            rows = pl.ds(64 * way, 64)
            first[p][way] = sent(pb.at[4, p, rows], rb.at[way, 0, p, rows], y_at(over[way]))

    def third_factor(rows, way, p):
        pb[3 + 2 * way, p] = partial(rows, p)
        moving[p][way] = sent(pb.at[3 + 2 * way, p], rb.at[way, 1, p], y_at(near[way]))

    far_factor(0)
    rows3 = take(1, 0)
    third_factor(rows3, 0, 0)
    rows5 = take(1, 1)
    third_factor(rows5, 1, 0)
    x_take(1)
    far_factor(1)
    third_factor(rows3, 0, 1)
    third_factor(rows5, 1, 1)
    for step in (2, 3):
        for way in range(2):
            slot = ((0, 1 + way), (1, 2 + way))[step - 2]
            rows = take(*slot)
            for p in range(2):
                pb[4 - step if way == 0 else 4 + step, p] = partial(rows, p)
        for p in range(2):
            for way in range(2):
                index = 4 - step if way == 0 else 4 + step
                moving[p][way].wait_recv()
                pb[index, p] += rb[way, step - 1, p]
                if step == 2:
                    first[p][way].wait_recv()
                    half_rows = slice(64 * way, 64 * way + 64)
                    pb[index, p, half_rows] += rb[way, 0, p, half_rows]
                moving[p][way] = sent(pb.at[index, p], rb.at[way, step, p], y_at(near[way]))
    rows0 = take(0, 3)
    for p in range(2):
        pb[0, p] = partial(rows0, p)
    convert(parity, x)

    def ring_send(p, step):
        made = []
        for way in range(2):
            index = ys((8 - step) % 8) if way == 0 else ys(step)
            if step == 2:
                ref = fg.at[index, p, pl.ds(64 * way, 64)]
                made.append(sent(ref, ref, y_at(over[way])))
            ref = fg.at[index, p]
            made.append(sent(ref, ref, y_at(near[way])))
        return made

    flips = [copy(fg.at[y, p], fy.at[y, p], at(x, z, y, h), keep=False) for p in range(2)]
    ring = [None, None]
    for p in range(2):
        for way in range(2):
            moving[p][way].wait_recv()
        fg[y, p] = pb[0, p] + rb[0, 3, p] + rb[1, 3, p]
        ring[p] = ring_send(p, 0)

    @pl.when(y != z)
    def _():
        for made in flips:
            made.start()

    @pl.when(y == z)
    def _():
        fy[z] = fg[y]

    for made in z_copies:
        made.wait_recv()
    high, low = split(jnp.concatenate([xz[src] for src in range(4)], axis=1))
    for p in range(2):
        gram[p] = partial((high, low), p)

    t_far = []
    for i in range(2):
        t_near[i].wait_recv()
        src = xs(3 - 2 * i)
        ref = tr.at[h, src, pl.ds(128 * i, 128)]
        t_far.append(sent(ref, ref, at(xs(1 + 2 * i), y, z, h)))
        ref = tr.at[h, src]
        t_cores.append(sent(ref, ref, at(x, y, z, other)))
    for p in range(2):
        for made in ring[p]:
            made.wait_recv()
        ring[p] = ring_send(p, 1)
    t_cores[0].wait_recv()
    convert(1 - parity, x)
    for i in range(2):
        convert(parity, xs(3 - 2 * i))
    for p in range(2):
        for made in ring[p]:
            made.wait_recv()
        ring[p] = ring_send(p, 2)

    def z_at(d):
        return at(x, y, zs(d), h)

    @pl.when(y != z)
    def _():
        for made in flips:
            made.wait_recv()

    second_near = [sent(fy.at[z], fy.at[z], z_at(near[way])) for way in range(2)]
    second_over = [sent(fy.at[z], fy.at[z], z_at(over[way])) for way in range(2)]
    for i in range(2):
        t_cores[1 + i].wait_recv()
        convert(1 - parity, xs(3 - 2 * i))
    t_last = []
    for i in range(2):
        t_far[i].wait_recv()
        ref = tr.at[h, xs(2), pl.ds(128 * i, 128)]
        t_last.append(sent(ref, ref, at(x, y, z, other)))
    convert(parity, xs(2))
    for made in t_last:
        made.wait_recv()
    convert(1 - parity, xs(2))

    pairs = ((0, 4), (1, 7), (2, 6), (3, 5))

    def image_part(p):
        for made in ring[p]:
            made.wait_recv()
        highs, lows = [], []
        for a, b in pairs:
            high, low = split(jnp.concatenate([fg[ys(a), p], fg[ys(b), p]], axis=1))
            highs.append(jnp.concatenate([high, low], axis=0))
            lows.append(high)
        for n in range(4):
            lanes = slice(256 * n, 256 * n + 256)
            total = None
            for i in range(4):
                both = dot_nt(highs[i], th[i, lanes, :])
                part = both[:128] + both[128:] + dot_nt(lows[i], tl[i, lanes, :])
                total = part if total is None else total + part
            acc[p, :, :, lanes] = total.reshape(8, 16, 256)

    def image_first(p):
        for way in range(2):
            rows = pl.ds(8 * way, 8)
            first[p][way] = sent(acc.at[p, zs(4), rows], rd.at[p, way, 0, rows], z_at(over[way]))
            moving[p][way] = sent(acc.at[p, zs(3 + 2 * way)], rd.at[p, way, 1], z_at(near[way]))

    def image_step(p, step):
        for way in range(2):
            index = zs(4 - step) if way == 0 else zs(4 + step)
            moving[p][way].wait_recv()
            acc[p, index] += rd[p, way, step - 1]
            if step == 2:
                first[p][way].wait_recv()
                rows = pl.ds(8 * way, 8)
                acc[p, index, rows] += rd[p, way, 0, rows]
            moving[p][way] = sent(acc.at[p, index], rd.at[p, way, step], z_at(near[way]))

    image_part(0)
    image_first(0)
    image_part(1)
    image_first(1)
    second_far = []
    for way in range(2):
        second_over[way].wait_recv()
        index = zs(6 - 4 * way)
        second_far.append(sent(fy.at[index], fy.at[index], z_at(near[way])))
        ref = fy.at[index, way]
        second_far.append(sent(ref, ref, z_at(over[way])))
    for step in (2, 3):
        for p in range(2):
            image_step(p, step)

    image_copies, out_copies = [], []
    for p in range(2):
        for made in moving[p]:
            made.wait_recv()
        total = acc[p, z] + rd[p, 0, 3] + rd[p, 1, 3]
        img[own, p] = total
        neg[p] = -total
        for px, ph in ((lax.rem(x + 1 - 2 * half + NX, NX), h), (lax.rem(x + 1 - 2 * half + NX, NX), other), (x, other)):
            made = copy(img.at[own, p], img.at[own, p], at(px, y, z, ph))
            made.start()
            image_copies.append(made)
    for p in range(2):
        for d in (1, 3, 2):
            to = xs(d)
            lanes = pl.ds(pl.multiple_of(256 * to, 256), 256)
            made = copy(neg.at[p, :, lanes], outr.at[x, p], at(to, y, z, h))
            made.start()
            out_copies.append(made)
        outr[x, p] = neg[p, :, pl.ds(pl.multiple_of(256 * x, 256), 256)]

    for made in second_near + second_far:
        made.wait_recv()
    for c in range(8):
        block = 4 * (c % 2) + c // 2
        high, low = split(fy[c].reshape(256, 128))
        fyh[:, 128 * block : 128 * block + 128] = high
        fyl[:, 128 * block : 128 * block + 128] = low

    for made in image_copies:
        made.wait_recv()
    high, low = split(img[...].reshape(128, 1024))
    ec[...] = (gram[...].reshape(256, 128) + dot3(fyh[...], fyl[...], high, low)).reshape(2, 8, 16, 128)
    e_copies = []
    for d in range(1, NY):
        made = copy(ec.at[:, ys(d)], er.at[d - 1], at(x, ys(d), z, h))
        made.start()
        e_copies.append(made)

    for made in out_copies:
        made.wait_recv()
    for src in range(4):
        for p in range(2):
            start = 32 * (src % 2) + 16 * p
            cross_ref[src // 2, start : start + 16] = outr[src, p]

    total = ec[:, y]
    for d in range(1, NY):
        e_copies[d - 1].wait_recv()
        total = total + er[d - 1]
    ch[...] = total.reshape(32, 128)

    def last(ph, sem):
        return pltpu.make_async_remote_copy(
            src_ref=ch, dst_ref=chr_.at[k], send_sem=last_sem.at[2 + sem], recv_sem=last_sem.at[k],
            device_id=at(own, y, z, ph), device_id_type=MESH,
        )

    last(other, 0).start()

    @pl.when(h != k)
    def _():
        last(h, 1).start()

    @pl.when(h == k)
    def _():
        chr_[k] = ch[...]

    def arrived(child):
        pltpu.make_async_remote_copy(
            src_ref=ch, dst_ref=chr_.at[child], send_sem=last_sem.at[2], recv_sem=last_sem.at[child],
            device_id=at(own, y, z, other), device_id_type=MESH,
        ).wait_recv()

    for child in range(2):
        @pl.when(jnp.logical_or(h != k, k != child))
        def _():
            arrived(child)

    @pl.when(h == 0)
    def _():
        child_ref[...] = chr_[:, :, :64]

    @pl.when(h == 1)
    def _():
        child_ref[...] = chr_[:, :, 64:]

    last(other, 0).wait_send()

    @pl.when(h != k)
    def _():
        last(h, 1).wait_send()

    @pl.when(y != z)
    def _():
        for made in flips:
            made.wait_send()

    for made in started:
        made.wait_send()


def local(top_inverse, coupling, child_inverse, tile_mask):
    vmem = pl.BlockSpec(memory_space=pltpu.VMEM)
    hbm = pl.BlockSpec(memory_space=pl.ANY)
    scratch = [
        pltpu.VMEM((2, 128, 1024), F32),
        pltpu.VMEM((2, 8, 128, 128), F32),
        pltpu.VMEM((2, 512, 128), F32),
        pltpu.VMEM((4, 2, 8, 16, 128), F32),
        pltpu.VMEM((4, 128, 128), F32),
        pltpu.VMEM((2, 4, 4, 128, 128), F32),
        pltpu.VMEM((2, 256, 512), BF16),
        pltpu.VMEM((2, 4, 256, 512), F32),
        pltpu.VMEM((4, 1024, 256), BF16),
        pltpu.VMEM((4, 1024, 256), BF16),
        pltpu.VMEM((8, 2, 128, 128), F32),
        pltpu.VMEM((2, 4, 2, 128, 128), F32),
        pltpu.VMEM((8, 2, 128, 128), F32),
        pltpu.VMEM((8, 2, 128, 128), F32),
        pltpu.VMEM((256, 1024), BF16),
        pltpu.VMEM((256, 1024), BF16),
        pltpu.VMEM((2, 8, 16, 1024), F32),
        pltpu.VMEM((2, 2, 4, 16, 1024), F32),
        pltpu.VMEM((4, 2, 16, 1024), F32),
        pltpu.VMEM((2, 16, 1024), F32),
        pltpu.VMEM((4, 2, 16, 256), F32),
        pltpu.VMEM((2, 8, 16, 128), F32),
        pltpu.VMEM((7, 2, 16, 128), F32),
        pltpu.VMEM((32, 128), F32),
        pltpu.VMEM((2, 32, 128), F32),
        pltpu.VMEM((2, 128, 128), F32),
        pltpu.SemaphoreType.DMA((NSEM,)),
        pltpu.SemaphoreType.DMA((NSEM,)),
        pltpu.SemaphoreType.DMA((4,)),
        pltpu.SemaphoreType.DMA((3,)),
    ]
    cross, child = pl.pallas_call(
        kernel,
        out_shape=(
            jax.ShapeDtypeStruct((2, 64, 256), F32),
            jax.ShapeDtypeStruct((2, 32, 64), F32),
        ),
        in_specs=[hbm, hbm, hbm, pl.BlockSpec(memory_space=pltpu.SMEM)],
        out_specs=(vmem, vmem),
        scratch_shapes=scratch,
        compiler_params=pltpu.CompilerParams(
            collective_id=0, has_side_effects=True, vmem_limit_bytes=48 << 20
        ),
        name="selected_inverse",
    )(top_inverse, coupling, child_inverse, tile_mask)
    return jnp.transpose(cross, (1, 0, 2)), jnp.transpose(child, (1, 0, 2))


def solution(mesh):
    in_specs = (P("row", "col"), P(None, "col", "row"), P(None, "row", None), P(None, "col"))
    out_specs = (P("col", None, "row"), P("row", None, "col"))
    return jax.shard_map(local, mesh=mesh, in_specs=in_specs, out_specs=out_specs, check_vma=False)
```

```python
import jax
import jax.numpy as jnp
from jax import lax
from jax.experimental import pallas as pl
from jax.experimental.pallas import tpu as pltpu
from jax.sharding import PartitionSpec as P


NX, NY, NZ = 4, 8, 8
MESH = pl.DeviceIdType.MESH
F32, BF16 = jnp.float32, jnp.bfloat16
NSEM = 160
EVEN = (4, 2, 6, 0)
ODD = (3, 5, 1, 7)


def split(value):
    high = value.astype(BF16)
    return high, (value - high.astype(F32)).astype(BF16)


def dot_nt(a, b):
    return lax.dot_general(a, b, (((1,), (1,)), ((), ())), preferred_element_type=F32)


def dot3(a_high, a_low, b_high, b_low):
    rows = a_high.shape[0]
    both = dot_nt(jnp.concatenate([a_high, a_low], axis=0), b_high)
    return both[:rows] + both[rows:] + dot_nt(a_high, b_low)


def kernel(
    top_ref, coupling_ref, inverse_ref, mask_ref, cross_ref, child_ref,
    xin, xt, masked, xr, xz, cr, xb, tr, th, tl, pb, rb, fg, fy, fyh, fyl,
    acc, rd, img, neg, outr, ec, er, ch, chr_, gram, send_sem, recv_sem, last_sem, load_sem,
):
    row, col = lax.axis_index("row"), lax.axis_index("col")
    x, y = lax.rem(row, NX), lax.div(row, NX)
    h, z = lax.rem(col, 2), lax.div(col, 2)
    k, half = lax.div(x, 2), lax.rem(x, 2)
    other = 1 - h
    parity = lax.rem(y + h, 2)
    own = 2 * h + half

    def at(px, py, pz, ph):
        return (py * NX + px, pz * 2 + ph)

    def xs(d):
        return lax.rem(x + d, NX)

    def ys(d):
        return lax.rem(y + d, NY)

    def zs(d):
        return lax.rem(z + d, NZ)

    started = []
    count = [0]

    def copy(src, dst, device, keep=True):
        i = count[0]
        count[0] += 1
        made = pltpu.make_async_remote_copy(
            src_ref=src, dst_ref=dst, send_sem=send_sem.at[i], recv_sem=recv_sem.at[i],
            device_id=device, device_id_type=MESH,
        )
        if keep:
            started.append(made)
        return made

    def sent(src, dst, device):
        made = copy(src, dst, device)
        made.start()
        return made

    loads = [
        pltpu.make_async_copy(inverse_ref, xin, load_sem.at[0]),
        pltpu.make_async_copy(coupling_ref, masked, load_sem.at[1]),
        pltpu.make_async_copy(top_ref, tr.at[h, x], load_sem.at[2]),
    ]
    for made in loads:
        made.start()
    barrier = pltpu.get_barrier_semaphore()

    def greet(device):
        pl.semaphore_signal(barrier, inc=1, device_id=device, device_id_type=MESH)

    for d in range(1, NX):
        greet(at(xs(d), y, z, h))
        greet(at(xs(d), y, z, other))
    greet(at(x, y, z, other))
    for d in range(1, NY):
        greet(at(x, ys(d), z, h))
    for d in (1, 2, 6, 7):
        greet(at(x, y, zs(d), h))

    @pl.when(y != z)
    def _():
        greet(at(x, z, y, h))

    loads[0].wait()
    for child in range(2):
        for s in range(8):
            xt[child, s] = xin[child, :, 128 * s : 128 * s + 128].T
    loads[1].wait()
    for child in range(2):
        for tile in range(2):
            number = mask_ref[child, tile].astype(F32)
            masked[child, 256 * tile : 256 * tile + 256] *= number

    @pl.when(y != z)
    def _():
        pl.semaphore_wait(barrier, 19)

    @pl.when(y == z)
    def _():
        pl.semaphore_wait(barrier, 18)

    def x_rows(to_half, p):
        return pl.ds(pl.multiple_of(64 * h + 32 * to_half + 16 * p, 16), 16)

    def x_send(p):
        made = []
        for d in (1, 3, 2):
            to = xs(d)
            made.append(
                copy(
                    xt.at[lax.div(to, 2), :, x_rows(lax.rem(to, 2), p), :],
                    xr.at[x, p],
                    at(to, y, z, h),
                )
            )
            made[-1].start()
        xr[x, p] = xt[k, :, x_rows(half, p), :]
        return made

    def chunk_rows(s):
        dist = EVEN[s] + parity * (ODD[s] - EVEN[s])
        sub = lax.div(ys(dist), 2)
        return pl.ds(pl.multiple_of(128 * sub, 128), 128)

    def c_send(s):
        made = []
        for d in (1, 3, 2):
            to = xs(d)
            made.append(
                copy(
                    masked.at[lax.div(to, 2), chunk_rows(s), :],
                    cr.at[parity, s, x],
                    at(to, y, z, h),
                )
            )
            made[-1].start()
        cr[parity, s, x] = masked[k, chunk_rows(s), :]
        return made

    x_copies = [x_send(0)]
    c_copies = [c_send(0)]
    x_copies.append(x_send(1))
    for s in range(1, 4):
        c_copies.append(c_send(s))
    forwards = [copy(cr.at[parity, s], cr.at[parity, s], at(x, y, z, other)) for s in range(4)]

    loads[2].wait()
    mine = tr.at[h, x]
    t_near = [copy(mine, mine, at(xs(d), y, z, h)) for d in (1, 3)]
    t_cores = [copy(mine, mine, at(x, y, z, other))]
    for made in t_near + t_cores:
        made.start()

    z_copies = []
    for d in (1, 3, 2):
        to = xs(d)
        z_copies.append(sent(xt.at[lax.div(to, 2), z], xz.at[x], at(to, y, z, h)))
    xz[x] = xt[k, z]

    def convert(which, src):
        core = lax.rem(y + which, 2)
        rows = pl.ds(pl.multiple_of(256 * src, 256), 256)
        for i in range(2):
            n = which + 2 * i
            for side in range(2):
                far = lax.rem(8 - n, 8) if side else n
                dist = jnp.where(n == 0, 4 * side, far)
                lanes = pl.ds(pl.multiple_of(128 * lax.div(ys(dist), 2), 128), 128)
                high, low = split(tr[core, src, :, lanes])
                th[n, rows, 128 * side : 128 * side + 128] = high
                tl[n, rows, 128 * side : 128 * side + 128] = low

    def x_take(p):
        for made in x_copies[p]:
            made.wait_recv()
        for src in range(4):
            high, low = split(xr[src, p].reshape(128, 128))
            lanes = slice(128 * src, 128 * src + 128)
            xb[p, :128, lanes] = high
            xb[p, 128:, lanes] = low

    def take(which, s):
        @pl.when(parity == which)
        def _():
            for made in c_copies[s]:
                made.wait_recv()
            forwards[s].start()

        @pl.when(parity != which)
        def _():
            forwards[s].wait_recv()

        return split(jnp.concatenate([cr[which, s, src] for src in range(4)], axis=1))

    def partial(rows, p):
        high, low = rows
        both = dot_nt(xb[p], high)
        return both[:128] + both[128:] + dot_nt(xb[p, :128], low)

    def y_at(d):
        return at(x, ys(d), z, h)

    near = (1, 7)
    over = (2, 6)
    x_take(0)
    rows4 = take(0, 0)
    first = [[None, None], [None, None]]
    moving = [[None, None], [None, None]]

    def far_factor(p):
        pb[4, p] = partial(rows4, p)
        for way in range(2):
            rows = pl.ds(64 * way, 64)
            first[p][way] = sent(pb.at[4, p, rows], rb.at[way, 0, p, rows], y_at(over[way]))

    def third_factor(rows, way, p):
        pb[3 + 2 * way, p] = partial(rows, p)
        moving[p][way] = sent(pb.at[3 + 2 * way, p], rb.at[way, 1, p], y_at(near[way]))

    far_factor(0)
    rows3 = take(1, 0)
    third_factor(rows3, 0, 0)
    rows5 = take(1, 1)
    third_factor(rows5, 1, 0)
    x_take(1)
    far_factor(1)
    third_factor(rows3, 0, 1)
    third_factor(rows5, 1, 1)
    for step in (2, 3):
        for way in range(2):
            slot = ((0, 1 + way), (1, 2 + way))[step - 2]
            rows = take(*slot)
            for p in range(2):
                pb[4 - step if way == 0 else 4 + step, p] = partial(rows, p)
        for p in range(2):
            for way in range(2):
                index = 4 - step if way == 0 else 4 + step
                moving[p][way].wait_recv()
                pb[index, p] += rb[way, step - 1, p]
                if step == 2:
                    first[p][way].wait_recv()
                    half_rows = slice(64 * way, 64 * way + 64)
                    pb[index, p, half_rows] += rb[way, 0, p, half_rows]
                moving[p][way] = sent(pb.at[index, p], rb.at[way, step, p], y_at(near[way]))
    rows0 = take(0, 3)
    for p in range(2):
        pb[0, p] = partial(rows0, p)
    convert(parity, x)

    def ring_send(p, step):
        made = []
        for way in range(2):
            index = ys((8 - step) % 8) if way == 0 else ys(step)
            if step == 2:
                ref = fg.at[index, p, pl.ds(64 * way, 64)]
                made.append(sent(ref, ref, y_at(over[way])))
            ref = fg.at[index, p]
            made.append(sent(ref, ref, y_at(near[way])))
        return made

    flips, flip_sems = [], []
    for p in range(2):
        flip_sems.append(count[0])
        flips.append(copy(fg.at[y, p], fy.at[y, p], at(x, z, y, h), keep=False))
    relays = []

    def relay(d, p):
        i = count[0]
        count[0] += 1
        relays.append(
            pltpu.make_async_remote_copy(
                src_ref=fg.at[ys(d), p], dst_ref=fy.at[ys(d), p], send_sem=send_sem.at[i],
                recv_sem=recv_sem.at[flip_sems[p]], device_id=at(x, y, zs(d), h),
                device_id_type=MESH,
            )
        )

        @pl.when(y == z)
        def _():
            relays[-1].start()

    ring = [None, None]
    for p in range(2):
        for way in range(2):
            moving[p][way].wait_recv()
        fg[y, p] = pb[0, p] + rb[0, 3, p] + rb[1, 3, p]
        ring[p] = ring_send(p, 0)

    apart = lax.rem(z - y + 8, 8)
    far_apart = y != z
    for d in near:
        far_apart = jnp.logical_and(far_apart, apart != d)

    @pl.when(far_apart)
    def _():
        for made in flips:
            made.start()

    @pl.when(y == z)
    def _():
        fy[z] = fg[y]

    for made in z_copies:
        made.wait_recv()
    high, low = split(jnp.concatenate([xz[src] for src in range(4)], axis=1))
    for p in range(2):
        gram[p] = partial((high, low), p)

    t_far = []
    for i in range(2):
        t_near[i].wait_recv()
        src = xs(3 - 2 * i)
        ref = tr.at[h, src, pl.ds(128 * i, 128)]
        t_far.append(sent(ref, ref, at(xs(1 + 2 * i), y, z, h)))
        ref = tr.at[h, src]
        t_cores.append(sent(ref, ref, at(x, y, z, other)))
    for p in range(2):
        for made in ring[p]:
            made.wait_recv()
        ring[p] = ring_send(p, 1)
        for d in near:
            relay(d, p)
    t_cores[0].wait_recv()
    convert(1 - parity, x)
    for i in range(2):
        convert(parity, xs(3 - 2 * i))
    for p in range(2):
        for made in ring[p]:
            made.wait_recv()
        ring[p] = ring_send(p, 2)

    def z_at(d):
        return at(x, y, zs(d), h)

    @pl.when(y != z)
    def _():
        for made in flips:
            made.wait_recv()

    def second_send(step):
        made = []
        for way in range(2):
            index = zs((8 - step) % 8) if way == 0 else zs(step)
            ref = fy.at[index, way] if step == 3 else fy.at[index]
            made.append(sent(ref, ref, z_at(near[way])))
        return made

    def second_next(step):
        for made in second[-1]:
            made.wait_recv()
        second.append(second_send(step))

    second = [second_send(0)]
    for i in range(2):
        t_cores[1 + i].wait_recv()
        convert(1 - parity, xs(3 - 2 * i))
    t_last = []
    for i in range(2):
        t_far[i].wait_recv()
        ref = tr.at[h, xs(2), pl.ds(128 * i, 128)]
        t_last.append(sent(ref, ref, at(x, y, z, other)))
    convert(parity, xs(2))
    for made in t_last:
        made.wait_recv()
    convert(1 - parity, xs(2))

    pairs = ((0, 4), (1, 7), (2, 6), (3, 5))

    def image_part(p):
        for made in ring[p]:
            made.wait_recv()
        highs, lows = [], []
        for a, b in pairs:
            high, low = split(jnp.concatenate([fg[ys(a), p], fg[ys(b), p]], axis=1))
            highs.append(jnp.concatenate([high, low], axis=0))
            lows.append(high)
        for n in range(4):
            lanes = slice(256 * n, 256 * n + 256)
            total = None
            for i in range(4):
                both = dot_nt(highs[i], th[i, lanes, :])
                part = both[:128] + both[128:] + dot_nt(lows[i], tl[i, lanes, :])
                total = part if total is None else total + part
            acc[p, :, :, lanes] = total.reshape(8, 16, 256)

    def image_first(p):
        for way in range(2):
            rows = pl.ds(8 * way, 8)
            first[p][way] = sent(acc.at[p, zs(4), rows], rd.at[p, way, 0, rows], z_at(over[way]))
            moving[p][way] = sent(acc.at[p, zs(3 + 2 * way)], rd.at[p, way, 1], z_at(near[way]))

    def image_step(p, step):
        for way in range(2):
            index = zs(4 - step) if way == 0 else zs(4 + step)
            moving[p][way].wait_recv()
            acc[p, index] += rd[p, way, step - 1]
            if step == 2:
                first[p][way].wait_recv()
                rows = pl.ds(8 * way, 8)
                acc[p, index, rows] += rd[p, way, 0, rows]
            moving[p][way] = sent(acc.at[p, index], rd.at[p, way, step], z_at(near[way]))

    image_part(0)
    image_first(0)
    image_part(1)
    image_first(1)
    for step in (2, 3):
        second_next(step - 1)
        for p in range(2):
            image_step(p, step)
    second_next(3)

    image_copies, image_cores, out_copies = [], [], []
    for p in range(2):
        for made in moving[p]:
            made.wait_recv()
        total = acc[p, z] + rd[p, 0, 3] + rd[p, 1, 3]
        img[own, p] = total
        neg[p] = -total
        pair = lax.rem(x + 1 - 2 * half + NX, NX)
        ref = img.at[own, p]
        image_copies.append(sent(ref, ref, at(pair, y, z, h)))
        image_cores.append(sent(ref, ref, at(x, y, z, other)))
    for p in range(2):
        for d in (1, 3, 2):
            to = xs(d)
            lanes = pl.ds(pl.multiple_of(256 * to, 256), 256)
            made = copy(neg.at[p, :, lanes], outr.at[x, p], at(to, y, z, h))
            made.start()
            out_copies.append(made)
        outr[x, p] = neg[p, :, pl.ds(pl.multiple_of(256 * x, 256), 256)]

    for made in second[-1]:
        made.wait_recv()
    for c in range(8):
        block = 4 * (c % 2) + c // 2
        high, low = split(fy[c].reshape(256, 128))
        fyh[:, 128 * block : 128 * block + 128] = high
        fyl[:, 128 * block : 128 * block + 128] = low

    for p in range(2):
        image_copies[p].wait_recv()
        ref = img.at[2 * h + 1 - half, p]
        image_cores.append(sent(ref, ref, at(x, y, z, other)))
    for made in image_cores:
        made.wait_recv()
    high, low = split(img[...].reshape(128, 1024))
    ec[...] = (gram[...].reshape(256, 128) + dot3(fyh[...], fyl[...], high, low)).reshape(2, 8, 16, 128)
    e_copies = []
    for d in (4, 3, 5, 2, 6, 1, 7):
        e_copies.append(sent(ec.at[:, ys(d)], er.at[d - 1], y_at(d)))

    for made in out_copies:
        made.wait_recv()
    for src in range(4):
        for p in range(2):
            start = 32 * (src % 2) + 16 * p
            cross_ref[src // 2, start : start + 16] = outr[src, p]

    for made in e_copies:
        made.wait_recv()
    total = ec[:, y]
    for d in range(1, NY):
        total = total + er[d - 1]
    ch[...] = total.reshape(32, 128)

    def last(ph, sem):
        return pltpu.make_async_remote_copy(
            src_ref=ch, dst_ref=chr_.at[k], send_sem=last_sem.at[2 + sem], recv_sem=last_sem.at[k],
            device_id=at(own, y, z, ph), device_id_type=MESH,
        )

    last(other, 0).start()

    @pl.when(h != k)
    def _():
        last(h, 1).start()

    @pl.when(h == k)
    def _():
        chr_[k] = ch[...]

    def arrived(child):
        pltpu.make_async_remote_copy(
            src_ref=ch, dst_ref=chr_.at[child], send_sem=last_sem.at[2], recv_sem=last_sem.at[child],
            device_id=at(own, y, z, other), device_id_type=MESH,
        ).wait_recv()

    for child in range(2):
        @pl.when(jnp.logical_or(h != k, k != child))
        def _():
            arrived(child)

    @pl.when(h == 0)
    def _():
        child_ref[...] = chr_[:, :, :64]

    @pl.when(h == 1)
    def _():
        child_ref[...] = chr_[:, :, 64:]

    last(other, 0).wait_send()

    @pl.when(h != k)
    def _():
        last(h, 1).wait_send()

    @pl.when(far_apart)
    def _():
        for made in flips:
            made.wait_send()

    @pl.when(y == z)
    def _():
        for made in relays:
            made.wait_send()

    for made in started:
        made.wait_send()


def local(top_inverse, coupling, child_inverse, tile_mask):
    vmem = pl.BlockSpec(memory_space=pltpu.VMEM)
    hbm = pl.BlockSpec(memory_space=pltpu.HBM)
    scratch = [
        pltpu.VMEM((2, 128, 1024), F32),
        pltpu.VMEM((2, 8, 128, 128), F32),
        pltpu.VMEM((2, 512, 128), F32),
        pltpu.VMEM((4, 2, 8, 16, 128), F32),
        pltpu.VMEM((4, 128, 128), F32),
        pltpu.VMEM((2, 4, 4, 128, 128), F32),
        pltpu.VMEM((2, 256, 512), BF16),
        pltpu.VMEM((2, 4, 256, 512), F32),
        pltpu.VMEM((4, 1024, 256), BF16),
        pltpu.VMEM((4, 1024, 256), BF16),
        pltpu.VMEM((8, 2, 128, 128), F32),
        pltpu.VMEM((2, 4, 2, 128, 128), F32),
        pltpu.VMEM((8, 2, 128, 128), F32),
        pltpu.VMEM((8, 2, 128, 128), F32),
        pltpu.VMEM((256, 1024), BF16),
        pltpu.VMEM((256, 1024), BF16),
        pltpu.VMEM((2, 8, 16, 1024), F32),
        pltpu.VMEM((2, 2, 4, 16, 1024), F32),
        pltpu.VMEM((4, 2, 16, 1024), F32),
        pltpu.VMEM((2, 16, 1024), F32),
        pltpu.VMEM((4, 2, 16, 256), F32),
        pltpu.VMEM((2, 8, 16, 128), F32),
        pltpu.VMEM((7, 2, 16, 128), F32),
        pltpu.VMEM((32, 128), F32),
        pltpu.VMEM((2, 32, 128), F32),
        pltpu.VMEM((2, 128, 128), F32),
        pltpu.SemaphoreType.DMA((NSEM,)),
        pltpu.SemaphoreType.DMA((NSEM,)),
        pltpu.SemaphoreType.DMA((4,)),
        pltpu.SemaphoreType.DMA((3,)),
    ]
    cross, child = pl.pallas_call(
        kernel,
        out_shape=(
            jax.ShapeDtypeStruct((2, 64, 256), F32),
            jax.ShapeDtypeStruct((2, 32, 64), F32),
        ),
        in_specs=[hbm, hbm, hbm, pl.BlockSpec(memory_space=pltpu.SMEM)],
        out_specs=(vmem, vmem),
        scratch_shapes=scratch,
        compiler_params=pltpu.CompilerParams(
            collective_id=0, has_side_effects=True, vmem_limit_bytes=60 << 20
        ),
        name="selected_inverse",
    )(top_inverse, coupling, child_inverse, tile_mask)
    return jnp.transpose(cross, (1, 0, 2)), jnp.transpose(child, (1, 0, 2))


def solution(mesh):
    in_specs = (P("row", "col"), P(None, "col", "row"), P(None, "row", None), P(None, "col"))
    out_specs = (P("col", None, "row"), P("row", None, "col"))
    return jax.shard_map(local, mesh=mesh, in_specs=in_specs, out_specs=out_specs, check_vma=False)
```

```python
import jax
import jax.numpy as jnp
from jax import lax
from jax.experimental import pallas as pl
from jax.experimental.pallas import tpu as pltpu
from jax.sharding import PartitionSpec as P


NX, NY, NZ = 4, 8, 8
MESH = pl.DeviceIdType.MESH
F32, BF16 = jnp.float32, jnp.bfloat16
NSEM = 160
EVEN = (4, 2, 6, 0)
ODD = (3, 5, 1, 7)


def split(value):
    high = value.astype(BF16)
    return high, (value - high.astype(F32)).astype(BF16)


def dot_nt(a, b):
    return lax.dot_general(a, b, (((1,), (1,)), ((), ())), preferred_element_type=F32)


def dot3(a_high, a_low, b_high, b_low):
    rows = a_high.shape[0]
    both = dot_nt(jnp.concatenate([a_high, a_low], axis=0), b_high)
    return both[:rows] + both[rows:] + dot_nt(a_high, b_low)


def kernel(
    top_ref, coupling_ref, inverse_ref, mask_ref, cross_ref, child_ref,
    xin, xt, masked, xr, xz, cr, xb, tr, th, tl, pb, rb, fg, fy, fyh, fyl,
    acc, rd, img, neg, outr, ec, er, gram, send_sem, recv_sem, last_sem, load_sem,
):
    row, col = lax.axis_index("row"), lax.axis_index("col")
    x, y = lax.rem(row, NX), lax.div(row, NX)
    h, z = lax.rem(col, 2), lax.div(col, 2)
    k, half = lax.div(x, 2), lax.rem(x, 2)
    other = 1 - h
    parity = lax.rem(y + h, 2)
    own = 2 * h + half

    def at(px, py, pz, ph):
        return (py * NX + px, pz * 2 + ph)

    def xs(d):
        return lax.rem(x + d, NX)

    def ys(d):
        return lax.rem(y + d, NY)

    def zs(d):
        return lax.rem(z + d, NZ)

    started = []
    count = [0]

    def copy(src, dst, device, keep=True):
        i = count[0]
        count[0] += 1
        made = pltpu.make_async_remote_copy(
            src_ref=src, dst_ref=dst, send_sem=send_sem.at[i], recv_sem=recv_sem.at[i],
            device_id=device, device_id_type=MESH,
        )
        if keep:
            started.append(made)
        return made

    def sent(src, dst, device):
        made = copy(src, dst, device)
        made.start()
        return made

    loads = [
        pltpu.make_async_copy(coupling_ref, masked, load_sem.at[0]),
        pltpu.make_async_copy(inverse_ref, xin, load_sem.at[1]),
        pltpu.make_async_copy(top_ref, tr.at[h, x], load_sem.at[2]),
    ]
    for made in loads:
        made.start()
    barrier = pltpu.get_barrier_semaphore()

    def greet(device):
        pl.semaphore_signal(barrier, inc=1, device_id=device, device_id_type=MESH)

    for d in range(1, NX):
        greet(at(xs(d), y, z, h))
        greet(at(xs(d), y, z, other))
    greet(at(x, y, z, other))
    for d in (1, 2, 6, 7):
        greet(at(x, ys(d), z, h))
    for d in range(1, NY):
        for child in range(2):
            greet(at(2 * child + half, ys(d), z, k))
    for d in (1, 2, 6, 7):
        greet(at(x, y, zs(d), h))

    @pl.when(y != z)
    def _():
        greet(at(x, z, y, h))

    loads[0].wait()
    for child in range(2):
        for tile in range(2):
            number = mask_ref[child, tile].astype(F32)
            masked[child, 256 * tile : 256 * tile + 256] *= number

    @pl.when(y != z)
    def _():
        pl.semaphore_wait(barrier, 30)

    @pl.when(y == z)
    def _():
        pl.semaphore_wait(barrier, 29)

    def x_rows(to_half, p):
        return pl.ds(pl.multiple_of(64 * h + 32 * to_half + 16 * p, 16), 16)

    def x_send(p):
        made = []
        for d in (1, 3, 2):
            to = xs(d)
            made.append(
                copy(
                    xt.at[lax.div(to, 2), :, x_rows(lax.rem(to, 2), p), :],
                    xr.at[x, p],
                    at(to, y, z, h),
                )
            )
            made[-1].start()
        xr[x, p] = xt[k, :, x_rows(half, p), :]
        return made

    def chunk_rows(s):
        dist = EVEN[s] + parity * (ODD[s] - EVEN[s])
        sub = lax.div(ys(dist), 2)
        return pl.ds(pl.multiple_of(128 * sub, 128), 128)

    def c_send(s):
        made = []
        for d in (1, 3, 2):
            to = xs(d)
            made.append(
                copy(
                    masked.at[lax.div(to, 2), chunk_rows(s), :],
                    cr.at[parity, s, x],
                    at(to, y, z, h),
                )
            )
            made[-1].start()
        cr[parity, s, x] = masked[k, chunk_rows(s), :]
        return made

    c_copies = [c_send(0)]
    loads[1].wait()
    for child in range(2):
        for s in range(8):
            xt[child, s] = xin[child, :, 128 * s : 128 * s + 128].T
    x_copies = [x_send(0), x_send(1)]
    for s in range(1, 4):
        c_copies.append(c_send(s))
    forwards = [copy(cr.at[parity, s], cr.at[parity, s], at(x, y, z, other)) for s in range(4)]

    loads[2].wait()
    mine = tr.at[h, x]
    t_near = [copy(mine, mine, at(xs(d), y, z, h)) for d in (1, 3)]
    t_cores = [copy(mine, mine, at(x, y, z, other))]
    for made in t_near + t_cores:
        made.start()

    z_copies = []
    for d in (1, 3, 2):
        to = xs(d)
        z_copies.append(sent(xt.at[lax.div(to, 2), z], xz.at[x], at(to, y, z, h)))
    xz[x] = xt[k, z]

    def convert(which, src):
        core = lax.rem(y + which, 2)
        rows = pl.ds(pl.multiple_of(256 * src, 256), 256)
        for i in range(2):
            n = which + 2 * i
            for side in range(2):
                far = lax.rem(8 - n, 8) if side else n
                dist = jnp.where(n == 0, 4 * side, far)
                lanes = pl.ds(pl.multiple_of(128 * lax.div(ys(dist), 2), 128), 128)
                high, low = split(tr[core, src, :, lanes])
                th[n, rows, 128 * side : 128 * side + 128] = high
                tl[n, rows, 128 * side : 128 * side + 128] = low

    def x_take(p):
        for made in x_copies[p]:
            made.wait_recv()
        for src in range(4):
            high, low = split(xr[src, p].reshape(128, 128))
            lanes = slice(128 * src, 128 * src + 128)
            xb[p, :128, lanes] = high
            xb[p, 128:, lanes] = low

    def take(which, s):
        @pl.when(parity == which)
        def _():
            for made in c_copies[s]:
                made.wait_recv()
            forwards[s].start()

        @pl.when(parity != which)
        def _():
            forwards[s].wait_recv()

        return split(jnp.concatenate([cr[which, s, src] for src in range(4)], axis=1))

    def partial(rows, p):
        high, low = rows
        both = dot_nt(xb[p], high)
        return both[:128] + both[128:] + dot_nt(xb[p, :128], low)

    def y_at(d):
        return at(x, ys(d), z, h)

    near = (1, 7)
    over = (2, 6)
    x_take(0)
    rows4 = take(0, 0)
    first = [[None, None], [None, None]]
    moving = [[None, None], [None, None]]

    def far_factor(p):
        pb[4, p] = partial(rows4, p)
        for way in range(2):
            rows = pl.ds(64 * way, 64)
            first[p][way] = sent(pb.at[4, p, rows], rb.at[way, 0, p, rows], y_at(over[way]))

    def third_factor(rows, way, p):
        pb[3 + 2 * way, p] = partial(rows, p)
        moving[p][way] = sent(pb.at[3 + 2 * way, p], rb.at[way, 1, p], y_at(near[way]))

    far_factor(0)
    rows3 = take(1, 0)
    third_factor(rows3, 0, 0)
    rows5 = take(1, 1)
    third_factor(rows5, 1, 0)
    x_take(1)
    far_factor(1)
    third_factor(rows3, 0, 1)
    third_factor(rows5, 1, 1)
    for step in (2, 3):
        taken = []
        for way in range(2):
            slot = ((0, 1 + way), (1, 2 + way))[step - 2]
            taken.append(take(*slot))
        for p in range(2):
            for way in range(2):
                pb[4 - step if way == 0 else 4 + step, p] = partial(taken[way], p)
            for way in range(2):
                index = 4 - step if way == 0 else 4 + step
                moving[p][way].wait_recv()
                pb[index, p] += rb[way, step - 1, p]
                if step == 2:
                    first[p][way].wait_recv()
                    half_rows = slice(64 * way, 64 * way + 64)
                    pb[index, p, half_rows] += rb[way, 0, p, half_rows]
                moving[p][way] = sent(pb.at[index, p], rb.at[way, step, p], y_at(near[way]))
    rows0 = take(0, 3)
    for p in range(2):
        pb[0, p] = partial(rows0, p)
    convert(parity, x)

    def ring_send(p, step):
        made = []
        for way in range(2):
            index = ys((8 - step) % 8) if way == 0 else ys(step)
            if step == 2:
                ref = fg.at[index, p, pl.ds(64 * way, 64)]
                made.append(sent(ref, ref, y_at(over[way])))
            ref = fg.at[index, p]
            made.append(sent(ref, ref, y_at(near[way])))
        return made

    flips, flip_sems = [], []
    for p in range(2):
        flip_sems.append(count[0])
        flips.append(copy(fg.at[y, p], fy.at[y, p], at(x, z, y, h), keep=False))
    relays = []

    def relay(d, p):
        i = count[0]
        count[0] += 1
        relays.append(
            pltpu.make_async_remote_copy(
                src_ref=fg.at[ys(d), p], dst_ref=fy.at[ys(d), p], send_sem=send_sem.at[i],
                recv_sem=recv_sem.at[flip_sems[p]], device_id=at(x, y, zs(d), h),
                device_id_type=MESH,
            )
        )

        @pl.when(y == z)
        def _():
            relays[-1].start()

    ring = [None, None]
    for p in range(2):
        for way in range(2):
            moving[p][way].wait_recv()
        fg[y, p] = pb[0, p] + rb[0, 3, p] + rb[1, 3, p]
        ring[p] = ring_send(p, 0)

    apart = lax.rem(z - y + 8, 8)
    far_apart = y != z
    for d in near + over:
        far_apart = jnp.logical_and(far_apart, apart != d)

    @pl.when(far_apart)
    def _():
        for made in flips:
            made.start()

    @pl.when(y == z)
    def _():
        fy[z] = fg[y]

    for made in z_copies:
        made.wait_recv()
    high, low = split(jnp.concatenate([xz[src] for src in range(4)], axis=1))
    for p in range(2):
        gram[p] = partial((high, low), p)

    t_far = []
    for i in range(2):
        t_near[i].wait_recv()
        src = xs(3 - 2 * i)
        ref = tr.at[h, src, pl.ds(128 * i, 128)]
        t_far.append(sent(ref, ref, at(xs(1 + 2 * i), y, z, h)))
        ref = tr.at[h, src]
        t_cores.append(sent(ref, ref, at(x, y, z, other)))
    for p in range(2):
        for made in ring[p]:
            made.wait_recv()
        ring[p] = ring_send(p, 1)
        for d in near:
            relay(d, p)
    t_cores[0].wait_recv()
    convert(1 - parity, x)
    for i in range(2):
        convert(parity, xs(3 - 2 * i))
    for p in range(2):
        for made in ring[p]:
            made.wait_recv()
        ring[p] = ring_send(p, 2)
        for d in over:
            relay(d, p)

    def z_at(d):
        return at(x, y, zs(d), h)

    @pl.when(y != z)
    def _():
        for made in flips:
            made.wait_recv()

    def second_send(step):
        made = []
        for way in range(2):
            index = zs((8 - step) % 8) if way == 0 else zs(step)
            ref = fy.at[index, way] if step == 3 else fy.at[index]
            made.append(sent(ref, ref, z_at(near[way])))
        return made

    def second_next(step):
        for made in second[-1]:
            made.wait_recv()
        second.append(second_send(step))

    second = [second_send(0)]
    for i in range(2):
        t_cores[1 + i].wait_recv()
        convert(1 - parity, xs(3 - 2 * i))
    t_last = []
    for i in range(2):
        t_far[i].wait_recv()
        ref = tr.at[h, xs(2), pl.ds(128 * i, 128)]
        t_last.append(sent(ref, ref, at(x, y, z, other)))
    convert(parity, xs(2))
    for made in t_last:
        made.wait_recv()
    convert(1 - parity, xs(2))

    pairs = ((0, 4), (1, 7), (2, 6), (3, 5))

    def image_part(p):
        for made in ring[p]:
            made.wait_recv()
        highs, lows = [], []
        for a, b in pairs:
            high, low = split(jnp.concatenate([fg[ys(a), p], fg[ys(b), p]], axis=1))
            highs.append(jnp.concatenate([high, low], axis=0))
            lows.append(high)
        for n in range(4):
            lanes = slice(256 * n, 256 * n + 256)
            total = None
            for i in range(4):
                both = dot_nt(highs[i], th[i, lanes, :])
                part = both[:128] + both[128:] + dot_nt(lows[i], tl[i, lanes, :])
                total = part if total is None else total + part
            acc[p, :, :, lanes] = total.reshape(8, 16, 256)

    def image_first(p):
        for way in range(2):
            rows = pl.ds(8 * way, 8)
            first[p][way] = sent(acc.at[p, zs(4), rows], rd.at[p, way, 0, rows], z_at(over[way]))
            moving[p][way] = sent(acc.at[p, zs(3 + 2 * way)], rd.at[p, way, 1], z_at(near[way]))

    def image_step(p, step):
        for way in range(2):
            index = zs(4 - step) if way == 0 else zs(4 + step)
            moving[p][way].wait_recv()
            acc[p, index] += rd[p, way, step - 1]
            if step == 2:
                first[p][way].wait_recv()
                rows = pl.ds(8 * way, 8)
                acc[p, index, rows] += rd[p, way, 0, rows]
            moving[p][way] = sent(acc.at[p, index], rd.at[p, way, step], z_at(near[way]))

    image_part(0)
    image_first(0)
    image_part(1)
    image_first(1)
    for step in (2, 3):
        second_next(step - 1)
        for p in range(2):
            image_step(p, step)
    second_next(3)

    image_copies, image_cores, out_copies = [], [], []
    for p in range(2):
        for made in moving[p]:
            made.wait_recv()
        total = acc[p, z] + rd[p, 0, 3] + rd[p, 1, 3]
        img[own, p] = total
        neg[p] = -total
        pair = lax.rem(x + 1 - 2 * half + NX, NX)
        ref = img.at[own, p]
        image_copies.append(sent(ref, ref, at(pair, y, z, h)))
        image_cores.append(sent(ref, ref, at(x, y, z, other)))
    for p in range(2):
        for d in (1, 3, 2):
            to = xs(d)
            lanes = pl.ds(pl.multiple_of(256 * to, 256), 256)
            made = copy(neg.at[p, :, lanes], outr.at[x, p], at(to, y, z, h))
            made.start()
            out_copies.append(made)
        outr[x, p] = neg[p, :, pl.ds(pl.multiple_of(256 * x, 256), 256)]

    for made in second[-1]:
        made.wait_recv()
    for c in range(8):
        block = 4 * (c % 2) + c // 2
        high, low = split(fy[c].reshape(256, 128))
        fyh[:, 128 * block : 128 * block + 128] = high
        fyl[:, 128 * block : 128 * block + 128] = low

    for p in range(2):
        image_copies[p].wait_recv()
        ref = img.at[2 * h + 1 - half, p]
        image_cores.append(sent(ref, ref, at(x, y, z, other)))
    for made in image_cores:
        made.wait_recv()
    high, low = split(img[...].reshape(128, 1024))
    total = gram[...].reshape(256, 128) + dot3(fyh[...], fyl[...], high, low)
    total = total.reshape(2, 8, 16, 128)
    for ph in range(2):
        lanes = slice(64 * ph, 64 * ph + 64)
        ec[ph] = jnp.concatenate([total[0, :, :, lanes], total[1, :, :, lanes]], axis=-1)

    def last(d, ph, i):
        return pltpu.make_async_remote_copy(
            src_ref=ec.at[ph, ys(d)], dst_ref=er.at[k, d], send_sem=last_sem.at[16 + i],
            recv_sem=last_sem.at[8 * k + d], device_id=at(own, ys(d), z, ph), device_id_type=MESH,
        )

    order = (4, 3, 5, 2, 6, 1, 7, 0)
    for d in order:
        last(d, other, 8 + d).start()
        if d:
            last(d, h, d).start()

    @pl.when(h != k)
    def _():
        last(0, h, 0).start()

    @pl.when(h == k)
    def _():
        er[k, 0] = ec[h, y]

    for made in out_copies:
        made.wait_recv()
    for src in range(4):
        for p in range(2):
            start = 32 * (src % 2) + 16 * p
            cross_ref[src // 2, start : start + 16] = outr[src, p]

    def arrived(child, d):
        pltpu.make_async_remote_copy(
            src_ref=ec.at[0, 0], dst_ref=er.at[child, d], send_sem=last_sem.at[16],
            recv_sem=last_sem.at[8 * child + d], device_id=at(own, y, z, other),
            device_id_type=MESH,
        ).wait_recv()

    for child in range(2):
        for d in range(1, NY):
            arrived(child, d)

        @pl.when(jnp.logical_or(h != k, k != child))
        def _():
            arrived(child, 0)

        total = er[child, 0]
        for d in range(1, NY):
            total = total + er[child, d]
        child_ref[child, :16] = total[:, :64]
        child_ref[child, 16:] = total[:, 64:]

    for d in order:
        last(d, other, 8 + d).wait_send()
        if d:
            last(d, h, d).wait_send()

    @pl.when(h != k)
    def _():
        last(0, h, 0).wait_send()

    @pl.when(far_apart)
    def _():
        for made in flips:
            made.wait_send()

    @pl.when(y == z)
    def _():
        for made in relays:
            made.wait_send()

    for made in started:
        made.wait_send()


def local(top_inverse, coupling, child_inverse, tile_mask):
    vmem = pl.BlockSpec(memory_space=pltpu.VMEM)
    hbm = pl.BlockSpec(memory_space=pltpu.HBM)
    scratch = [
        pltpu.VMEM((2, 128, 1024), F32),
        pltpu.VMEM((2, 8, 128, 128), F32),
        pltpu.VMEM((2, 512, 128), F32),
        pltpu.VMEM((4, 2, 8, 16, 128), F32),
        pltpu.VMEM((4, 128, 128), F32),
        pltpu.VMEM((2, 4, 4, 128, 128), F32),
        pltpu.VMEM((2, 256, 512), BF16),
        pltpu.VMEM((2, 4, 256, 512), F32),
        pltpu.VMEM((4, 1024, 256), BF16),
        pltpu.VMEM((4, 1024, 256), BF16),
        pltpu.VMEM((8, 2, 128, 128), F32),
        pltpu.VMEM((2, 4, 2, 128, 128), F32),
        pltpu.VMEM((8, 2, 128, 128), F32),
        pltpu.VMEM((8, 2, 128, 128), F32),
        pltpu.VMEM((256, 1024), BF16),
        pltpu.VMEM((256, 1024), BF16),
        pltpu.VMEM((2, 8, 16, 1024), F32),
        pltpu.VMEM((2, 2, 4, 16, 1024), F32),
        pltpu.VMEM((4, 2, 16, 1024), F32),
        pltpu.VMEM((2, 16, 1024), F32),
        pltpu.VMEM((4, 2, 16, 256), F32),
        pltpu.VMEM((2, 8, 16, 128), F32),
        pltpu.VMEM((2, 8, 16, 128), F32),
        pltpu.VMEM((2, 128, 128), F32),
        pltpu.SemaphoreType.DMA((NSEM,)),
        pltpu.SemaphoreType.DMA((NSEM,)),
        pltpu.SemaphoreType.DMA((32,)),
        pltpu.SemaphoreType.DMA((3,)),
    ]
    cross, child = pl.pallas_call(
        kernel,
        out_shape=(
            jax.ShapeDtypeStruct((2, 64, 256), F32),
            jax.ShapeDtypeStruct((2, 32, 64), F32),
        ),
        in_specs=[hbm, hbm, hbm, pl.BlockSpec(memory_space=pltpu.SMEM)],
        out_specs=(vmem, vmem),
        scratch_shapes=scratch,
        compiler_params=pltpu.CompilerParams(
            collective_id=0, has_side_effects=True, vmem_limit_bytes=60 << 20
        ),
        name="selected_inverse",
    )(top_inverse, coupling, child_inverse, tile_mask)
    return jnp.transpose(cross, (1, 0, 2)), jnp.transpose(child, (1, 0, 2))


def solution(mesh):
    in_specs = (P("row", "col"), P(None, "col", "row"), P(None, "row", None), P(None, "col"))
    out_specs = (P("col", None, "row"), P("row", None, "col"))
    return jax.shard_map(local, mesh=mesh, in_specs=in_specs, out_specs=out_specs, check_vma=False)
```

```python
import jax
import jax.numpy as jnp
from jax import lax
from jax.experimental import pallas as pl
from jax.experimental.pallas import tpu as pltpu
from jax.sharding import PartitionSpec as P


NX, NY, NZ = 4, 8, 8
MESH = pl.DeviceIdType.MESH
F32, BF16 = jnp.float32, jnp.bfloat16
NSEM = 160
EVEN = (4, 2, 6, 0)
ODD = (3, 5, 1, 7)


def split(value):
    high = value.astype(BF16)
    return high, (value - high.astype(F32)).astype(BF16)


def dot_nt(a, b):
    return lax.dot_general(a, b, (((1,), (1,)), ((), ())), preferred_element_type=F32)


def dot3(a_high, a_low, b_high, b_low):
    rows = a_high.shape[0]
    both = dot_nt(jnp.concatenate([a_high, a_low], axis=0), b_high)
    return both[:rows] + both[rows:] + dot_nt(a_high, b_low)


def kernel(
    top_ref, coupling_ref, inverse_ref, mask_ref, cross_ref, child_ref,
    xin, xt, masked, xr, xz, cr, xb, tr, th, tl, pb, rb, fg, fy, fyh, fyl,
    acc, rd, img, neg, outr, ec, er, gram, send_sem, recv_sem, last_sem, load_sem,
):
    row, col = lax.axis_index("row"), lax.axis_index("col")
    x, y = lax.rem(row, NX), lax.div(row, NX)
    h, z = lax.rem(col, 2), lax.div(col, 2)
    k, half = lax.div(x, 2), lax.rem(x, 2)
    other = 1 - h
    parity = lax.rem(y + h, 2)
    own = 2 * h + half

    def at(px, py, pz, ph):
        return (py * NX + px, pz * 2 + ph)

    def xs(d):
        return lax.rem(x + d, NX)

    def ys(d):
        return lax.rem(y + d, NY)

    def zs(d):
        return lax.rem(z + d, NZ)

    started = []
    count = [0]

    def copy(src, dst, device, keep=True):
        i = count[0]
        count[0] += 1
        made = pltpu.make_async_remote_copy(
            src_ref=src, dst_ref=dst, send_sem=send_sem.at[i], recv_sem=recv_sem.at[i],
            device_id=device, device_id_type=MESH,
        )
        if keep:
            started.append(made)
        return made

    def sent(src, dst, device):
        made = copy(src, dst, device)
        made.start()
        return made

    loads = [
        pltpu.make_async_copy(coupling_ref, masked, load_sem.at[0]),
        pltpu.make_async_copy(inverse_ref, xin, load_sem.at[1]),
        pltpu.make_async_copy(top_ref, tr.at[h, x], load_sem.at[2]),
    ]
    for made in loads:
        made.start()
    barrier = pltpu.get_barrier_semaphore()

    def greet(device):
        pl.semaphore_signal(barrier, inc=1, device_id=device, device_id_type=MESH)

    for d in range(1, NX):
        greet(at(xs(d), y, z, h))
        greet(at(xs(d), y, z, other))
    greet(at(x, y, z, other))
    for d in (1, 2, 6, 7):
        greet(at(x, ys(d), z, h))
    for d in range(1, NY):
        for child in range(2):
            greet(at(2 * child + half, ys(d), z, k))
    for d in (1, 2, 6, 7):
        greet(at(x, y, zs(d), h))

    @pl.when(y != z)
    def _():
        greet(at(x, z, y, h))

    loads[0].wait()
    for child in range(2):
        for tile in range(2):
            number = mask_ref[child, tile].astype(F32)
            masked[child, 256 * tile : 256 * tile + 256] *= number

    @pl.when(y != z)
    def _():
        pl.semaphore_wait(barrier, 30)

    @pl.when(y == z)
    def _():
        pl.semaphore_wait(barrier, 29)

    def x_rows(to_half, p):
        return pl.ds(pl.multiple_of(64 * h + 32 * to_half + 16 * p, 16), 16)

    def x_send(p):
        made = []
        for d in (1, 3, 2):
            to = xs(d)
            made.append(
                copy(
                    xt.at[lax.div(to, 2), :, x_rows(lax.rem(to, 2), p), :],
                    xr.at[x, p],
                    at(to, y, z, h),
                )
            )
            made[-1].start()
        xr[x, p] = xt[k, :, x_rows(half, p), :]
        return made

    def chunk_rows(s):
        dist = EVEN[s] + parity * (ODD[s] - EVEN[s])
        sub = lax.div(ys(dist), 2)
        return pl.ds(pl.multiple_of(128 * sub, 128), 128)

    def c_send(s):
        made = []
        for d in (1, 3, 2):
            to = xs(d)
            made.append(
                copy(
                    masked.at[lax.div(to, 2), chunk_rows(s), :],
                    cr.at[parity, s, x],
                    at(to, y, z, h),
                )
            )
            made[-1].start()
        cr[parity, s, x] = masked[k, chunk_rows(s), :]
        return made

    c_copies = [c_send(0)]
    loads[1].wait()
    for child in range(2):
        for s in range(8):
            xt[child, s] = xin[child, :, 128 * s : 128 * s + 128].T
    x_copies = [x_send(0), x_send(1)]
    for s in range(1, 4):
        c_copies.append(c_send(s))
    forwards = [copy(cr.at[parity, s], cr.at[parity, s], at(x, y, z, other)) for s in range(4)]

    loads[2].wait()
    mine = tr.at[h, x]
    t_near = [copy(mine, mine, at(xs(d), y, z, h)) for d in (1, 3)]
    t_cores = [copy(mine, mine, at(x, y, z, other))]
    for made in t_near + t_cores:
        made.start()

    z_copies = []
    for d in (1, 3, 2):
        to = xs(d)
        z_copies.append(sent(xt.at[lax.div(to, 2), z], xz.at[x], at(to, y, z, h)))
    xz[x] = xt[k, z]

    def convert(which, src):
        core = lax.rem(y + which, 2)
        rows = pl.ds(pl.multiple_of(256 * src, 256), 256)
        for i in range(2):
            n = which + 2 * i
            for side in range(2):
                far = lax.rem(8 - n, 8) if side else n
                dist = jnp.where(n == 0, 4 * side, far)
                lanes = pl.ds(pl.multiple_of(128 * lax.div(ys(dist), 2), 128), 128)
                high, low = split(tr[core, src, :, lanes])
                th[n, rows, 128 * side : 128 * side + 128] = high
                tl[n, rows, 128 * side : 128 * side + 128] = low

    def x_take(p):
        for made in x_copies[p]:
            made.wait_recv()
        for src in range(4):
            high, low = split(xr[src, p].reshape(128, 128))
            lanes = slice(128 * src, 128 * src + 128)
            xb[p, :128, lanes] = high
            xb[p, 128:, lanes] = low

    def take(which, s):
        @pl.when(parity == which)
        def _():
            for made in c_copies[s]:
                made.wait_recv()
            forwards[s].start()

        @pl.when(parity != which)
        def _():
            forwards[s].wait_recv()

        return split(jnp.concatenate([cr[which, s, src] for src in range(4)], axis=1))

    def partial(rows, p):
        high, low = rows
        both = dot_nt(xb[p], high)
        return both[:128] + both[128:] + dot_nt(xb[p, :128], low)

    def y_at(d):
        return at(x, ys(d), z, h)

    near = (1, 7)
    over = (2, 6)
    x_take(0)
    rows4 = take(0, 0)
    first = [[None, None], [None, None]]
    moving = [[None, None], [None, None]]

    def far_factor(p):
        pb[4, p] = partial(rows4, p)
        for way in range(2):
            rows = pl.ds(64 * way, 64)
            first[p][way] = sent(pb.at[4, p, rows], rb.at[way, 0, p, rows], y_at(over[way]))

    def third_factor(rows, way, p):
        pb[3 + 2 * way, p] = partial(rows, p)
        moving[p][way] = sent(pb.at[3 + 2 * way, p], rb.at[way, 1, p], y_at(near[way]))

    far_factor(0)
    rows3 = take(1, 0)
    third_factor(rows3, 0, 0)
    rows5 = take(1, 1)
    third_factor(rows5, 1, 0)
    x_take(1)
    far_factor(1)
    third_factor(rows3, 0, 1)
    third_factor(rows5, 1, 1)
    for step in (2, 3):
        taken = []
        for way in range(2):
            slot = ((0, 1 + way), (1, 2 + way))[step - 2]
            taken.append(take(*slot))
        for p in range(2):
            for way in range(2):
                pb[4 - step if way == 0 else 4 + step, p] = partial(taken[way], p)
            for way in range(2):
                index = 4 - step if way == 0 else 4 + step
                moving[p][way].wait_recv()
                pb[index, p] += rb[way, step - 1, p]
                if step == 2:
                    first[p][way].wait_recv()
                    half_rows = slice(64 * way, 64 * way + 64)
                    pb[index, p, half_rows] += rb[way, 0, p, half_rows]
                moving[p][way] = sent(pb.at[index, p], rb.at[way, step, p], y_at(near[way]))
    rows0 = take(0, 3)
    for p in range(2):
        pb[0, p] = partial(rows0, p)
    convert(parity, x)

    def ring_send(p, step):
        made = []
        for way in range(2):
            index = ys((8 - step) % 8) if way == 0 else ys(step)
            if step == 2:
                ref = fg.at[index, p, pl.ds(64 * way, 64)]
                made.append(sent(ref, ref, y_at(over[way])))
            ref = fg.at[index, p]
            made.append(sent(ref, ref, y_at(near[way])))
        return made

    flips, flip_sems = [], []
    for p in range(2):
        flip_sems.append(count[0])
        flips.append(copy(fg.at[y, p], fy.at[y, p], at(x, z, y, h), keep=False))
    relays = []

    def relay(d, p):
        i = count[0]
        count[0] += 1
        relays.append(
            pltpu.make_async_remote_copy(
                src_ref=fg.at[ys(d), p], dst_ref=fy.at[ys(d), p], send_sem=send_sem.at[i],
                recv_sem=recv_sem.at[flip_sems[p]], device_id=at(x, y, zs(d), h),
                device_id_type=MESH,
            )
        )

        @pl.when(y == z)
        def _():
            relays[-1].start()

    apart = lax.rem(z - y + 8, 8)
    far_apart = y != z
    for d in near + over:
        far_apart = jnp.logical_and(far_apart, apart != d)

    def flip_start(made):
        @pl.when(far_apart)
        def _():
            made.start()

    ring = [None, None]
    for p in range(2):
        for way in range(2):
            moving[p][way].wait_recv()
        fg[y, p] = pb[0, p] + rb[0, 3, p] + rb[1, 3, p]
        ring[p] = ring_send(p, 0)
        flip_start(flips[p])

    @pl.when(y == z)
    def _():
        fy[z] = fg[y]

    for made in z_copies:
        made.wait_recv()
    high, low = split(jnp.concatenate([xz[src] for src in range(4)], axis=1))
    for p in range(2):
        gram[p] = partial((high, low), p)

    t_far = []
    for i in range(2):
        t_near[i].wait_recv()
        src = xs(3 - 2 * i)
        ref = tr.at[h, src, pl.ds(128 * i, 128)]
        t_far.append(sent(ref, ref, at(xs(1 + 2 * i), y, z, h)))
        ref = tr.at[h, src]
        t_cores.append(sent(ref, ref, at(x, y, z, other)))
    for p in range(2):
        for made in ring[p]:
            made.wait_recv()
        ring[p] = ring_send(p, 1)
        for d in near:
            relay(d, p)
    t_cores[0].wait_recv()
    convert(1 - parity, x)
    for i in range(2):
        convert(parity, xs(3 - 2 * i))
    for p in range(2):
        for made in ring[p]:
            made.wait_recv()
        ring[p] = ring_send(p, 2)
        for d in over:
            relay(d, p)

    def z_at(d):
        return at(x, y, zs(d), h)

    @pl.when(y != z)
    def _():
        for made in flips:
            made.wait_recv()

    def second_send(step):
        made = []
        for way in range(2):
            index = zs((8 - step) % 8) if way == 0 else zs(step)
            ref = fy.at[index, way] if step == 3 else fy.at[index]
            made.append(sent(ref, ref, z_at(near[way])))
        return made

    def second_next(step):
        for made in second[-1]:
            made.wait_recv()
        second.append(second_send(step))

    second = [second_send(0)]
    for i in range(2):
        t_cores[1 + i].wait_recv()
        convert(1 - parity, xs(3 - 2 * i))
    t_last = []
    for i in range(2):
        t_far[i].wait_recv()
        ref = tr.at[h, xs(2), pl.ds(128 * i, 128)]
        t_last.append(sent(ref, ref, at(x, y, z, other)))
    convert(parity, xs(2))
    for made in t_last:
        made.wait_recv()
    convert(1 - parity, xs(2))

    pairs = ((0, 4), (1, 7), (2, 6), (3, 5))

    def image_part(p):
        for made in ring[p]:
            made.wait_recv()
        highs, lows = [], []
        for a, b in pairs:
            high, low = split(jnp.concatenate([fg[ys(a), p], fg[ys(b), p]], axis=1))
            highs.append(jnp.concatenate([high, low], axis=0))
            lows.append(high)
        for n in range(4):
            lanes = slice(256 * n, 256 * n + 256)
            total = None
            for i in range(4):
                both = dot_nt(highs[i], th[i, lanes, :])
                part = both[:128] + both[128:] + dot_nt(lows[i], tl[i, lanes, :])
                total = part if total is None else total + part
            acc[p, :, :, lanes] = total.reshape(8, 16, 256)

    def image_first(p):
        for way in range(2):
            rows = pl.ds(8 * way, 8)
            first[p][way] = sent(acc.at[p, zs(4), rows], rd.at[p, way, 0, rows], z_at(over[way]))
            moving[p][way] = sent(acc.at[p, zs(3 + 2 * way)], rd.at[p, way, 1], z_at(near[way]))

    def image_step(p, step):
        for way in range(2):
            index = zs(4 - step) if way == 0 else zs(4 + step)
            moving[p][way].wait_recv()
            acc[p, index] += rd[p, way, step - 1]
            if step == 2:
                first[p][way].wait_recv()
                rows = pl.ds(8 * way, 8)
                acc[p, index, rows] += rd[p, way, 0, rows]
            moving[p][way] = sent(acc.at[p, index], rd.at[p, way, step], z_at(near[way]))

    image_part(0)
    image_first(0)
    image_part(1)
    image_first(1)
    for step in (2, 3):
        second_next(step - 1)
        for p in range(2):
            image_step(p, step)
    second_next(3)

    image_copies, image_cores, out_copies = [], [], []
    for p in range(2):
        for made in moving[p]:
            made.wait_recv()
        total = acc[p, z] + rd[p, 0, 3] + rd[p, 1, 3]
        img[own, p] = total
        neg[p] = -total
        pair = lax.rem(x + 1 - 2 * half + NX, NX)
        ref = img.at[own, p]
        image_copies.append(sent(ref, ref, at(pair, y, z, h)))
        image_cores.append(sent(ref, ref, at(x, y, z, other)))
    for p in range(2):
        for d in (1, 3, 2):
            to = xs(d)
            lanes = pl.ds(pl.multiple_of(256 * to, 256), 256)
            made = copy(neg.at[p, :, lanes], outr.at[x, p], at(to, y, z, h))
            made.start()
            out_copies.append(made)
        outr[x, p] = neg[p, :, pl.ds(pl.multiple_of(256 * x, 256), 256)]

    for made in second[-1]:
        made.wait_recv()
    for c in range(8):
        block = 4 * (c % 2) + c // 2
        high, low = split(fy[c].reshape(256, 128))
        fyh[:, 128 * block : 128 * block + 128] = high
        fyl[:, 128 * block : 128 * block + 128] = low

    for p in range(2):
        image_copies[p].wait_recv()
        ref = img.at[2 * h + 1 - half, p]
        image_cores.append(sent(ref, ref, at(x, y, z, other)))
    for made in image_cores:
        made.wait_recv()
    high, low = split(img[...].reshape(128, 1024))
    total = gram[...].reshape(256, 128) + dot3(fyh[...], fyl[...], high, low)
    total = total.reshape(2, 8, 16, 128)
    for ph in range(2):
        lanes = slice(64 * ph, 64 * ph + 64)
        ec[ph] = jnp.concatenate([total[0, :, :, lanes], total[1, :, :, lanes]], axis=-1)

    def last(d, ph, i):
        return pltpu.make_async_remote_copy(
            src_ref=ec.at[ph, ys(d)], dst_ref=er.at[k, d], send_sem=last_sem.at[16 + i],
            recv_sem=last_sem.at[8 * k + d], device_id=at(own, ys(d), z, ph), device_id_type=MESH,
        )

    order = (4, 3, 5, 2, 6, 1, 7, 0)
    for d in order:
        last(d, other, 8 + d).start()
        if d:
            last(d, h, d).start()

    @pl.when(h != k)
    def _():
        last(0, h, 0).start()

    @pl.when(h == k)
    def _():
        er[k, 0] = ec[h, y]

    for made in out_copies:
        made.wait_recv()
    for src in range(4):
        for p in range(2):
            start = 32 * (src % 2) + 16 * p
            cross_ref[src // 2, start : start + 16] = outr[src, p]

    def arrived(child, d):
        pltpu.make_async_remote_copy(
            src_ref=ec.at[0, 0], dst_ref=er.at[child, d], send_sem=last_sem.at[16],
            recv_sem=last_sem.at[8 * child + d], device_id=at(own, y, z, other),
            device_id_type=MESH,
        ).wait_recv()

    for child in range(2):
        for d in range(1, NY):
            arrived(child, d)

        @pl.when(jnp.logical_or(h != k, k != child))
        def _():
            arrived(child, 0)

        total = er[child, 0]
        for d in range(1, NY):
            total = total + er[child, d]
        child_ref[child, :16] = total[:, :64]
        child_ref[child, 16:] = total[:, 64:]

    for d in order:
        last(d, other, 8 + d).wait_send()
        if d:
            last(d, h, d).wait_send()

    @pl.when(h != k)
    def _():
        last(0, h, 0).wait_send()

    @pl.when(far_apart)
    def _():
        for made in flips:
            made.wait_send()

    @pl.when(y == z)
    def _():
        for made in relays:
            made.wait_send()

    for made in started:
        made.wait_send()


def local(top_inverse, coupling, child_inverse, tile_mask):
    vmem = pl.BlockSpec(memory_space=pltpu.VMEM)
    hbm = pl.BlockSpec(memory_space=pltpu.HBM)
    scratch = [
        pltpu.VMEM((2, 128, 1024), F32),
        pltpu.VMEM((2, 8, 128, 128), F32),
        pltpu.VMEM((2, 512, 128), F32),
        pltpu.VMEM((4, 2, 8, 16, 128), F32),
        pltpu.VMEM((4, 128, 128), F32),
        pltpu.VMEM((2, 4, 4, 128, 128), F32),
        pltpu.VMEM((2, 256, 512), BF16),
        pltpu.VMEM((2, 4, 256, 512), F32),
        pltpu.VMEM((4, 1024, 256), BF16),
        pltpu.VMEM((4, 1024, 256), BF16),
        pltpu.VMEM((8, 2, 128, 128), F32),
        pltpu.VMEM((2, 4, 2, 128, 128), F32),
        pltpu.VMEM((8, 2, 128, 128), F32),
        pltpu.VMEM((8, 2, 128, 128), F32),
        pltpu.VMEM((256, 1024), BF16),
        pltpu.VMEM((256, 1024), BF16),
        pltpu.VMEM((2, 8, 16, 1024), F32),
        pltpu.VMEM((2, 2, 4, 16, 1024), F32),
        pltpu.VMEM((4, 2, 16, 1024), F32),
        pltpu.VMEM((2, 16, 1024), F32),
        pltpu.VMEM((4, 2, 16, 256), F32),
        pltpu.VMEM((2, 8, 16, 128), F32),
        pltpu.VMEM((2, 8, 16, 128), F32),
        pltpu.VMEM((2, 128, 128), F32),
        pltpu.SemaphoreType.DMA((NSEM,)),
        pltpu.SemaphoreType.DMA((NSEM,)),
        pltpu.SemaphoreType.DMA((32,)),
        pltpu.SemaphoreType.DMA((3,)),
    ]
    cross, child = pl.pallas_call(
        kernel,
        out_shape=(
            jax.ShapeDtypeStruct((2, 64, 256), F32),
            jax.ShapeDtypeStruct((2, 32, 64), F32),
        ),
        in_specs=[hbm, hbm, hbm, pl.BlockSpec(memory_space=pltpu.SMEM)],
        out_specs=(vmem, vmem),
        scratch_shapes=scratch,
        compiler_params=pltpu.CompilerParams(
            collective_id=0, has_side_effects=True, vmem_limit_bytes=60 << 20
        ),
        name="selected_inverse",
    )(top_inverse, coupling, child_inverse, tile_mask)
    return jnp.transpose(cross, (1, 0, 2)), jnp.transpose(child, (1, 0, 2))


def solution(mesh):
    in_specs = (P("row", "col"), P(None, "col", "row"), P(None, "row", None), P(None, "col"))
    out_specs = (P("col", None, "row"), P("row", None, "col"))
    return jax.shard_map(local, mesh=mesh, in_specs=in_specs, out_specs=out_specs, check_vma=False)
```

```python
import jax
import jax.numpy as jnp
from jax import lax
from jax.experimental import pallas as pl
from jax.experimental.pallas import tpu as pltpu
from jax.sharding import PartitionSpec as P


NX, NY, NZ = 4, 8, 8
MESH = pl.DeviceIdType.MESH
F32, BF16 = jnp.float32, jnp.bfloat16
NSEM = 160
EVEN = (4, 2, 6, 0)
ODD = (3, 5, 1, 7)


def split(value):
    high = value.astype(BF16)
    return high, (value - high.astype(F32)).astype(BF16)


def dot_nt(a, b):
    return lax.dot_general(a, b, (((1,), (1,)), ((), ())), preferred_element_type=F32)


def dot3(a_high, a_low, b_high, b_low):
    rows = a_high.shape[0]
    both = dot_nt(jnp.concatenate([a_high, a_low], axis=0), b_high)
    return both[:rows] + both[rows:] + dot_nt(a_high, b_low)


def kernel(
    top_ref, coupling_ref, inverse_ref, mask_ref, cross_ref, child_ref,
    xin, xt, masked, xr, xz, cr, xb, tr, th, tl, pb, rb, fg, fy, fyh, fyl,
    acc, rd, img, neg, outr, ec, er, gram, send_sem, recv_sem, last_sem, load_sem,
):
    row, col = lax.axis_index("row"), lax.axis_index("col")
    x, y = lax.rem(row, NX), lax.div(row, NX)
    h, z = lax.rem(col, 2), lax.div(col, 2)
    k, half = lax.div(x, 2), lax.rem(x, 2)
    other = 1 - h
    parity = lax.rem(y + h, 2)
    own = 2 * h + half

    def at(px, py, pz, ph):
        return (py * NX + px, pz * 2 + ph)

    def xs(d):
        return lax.rem(x + d, NX)

    def ys(d):
        return lax.rem(y + d, NY)

    def zs(d):
        return lax.rem(z + d, NZ)

    started = []
    count = [0]

    def copy(src, dst, device, keep=True):
        i = count[0]
        count[0] += 1
        made = pltpu.make_async_remote_copy(
            src_ref=src, dst_ref=dst, send_sem=send_sem.at[i], recv_sem=recv_sem.at[i],
            device_id=device, device_id_type=MESH,
        )
        if keep:
            started.append(made)
        return made

    def sent(src, dst, device):
        made = copy(src, dst, device)
        made.start()
        return made

    loads = [
        pltpu.make_async_copy(coupling_ref, masked, load_sem.at[0]),
        pltpu.make_async_copy(inverse_ref, xin, load_sem.at[1]),
        pltpu.make_async_copy(top_ref, tr.at[h, x], load_sem.at[2]),
    ]
    for made in loads:
        made.start()
    barrier = pltpu.get_barrier_semaphore()

    def greet(device):
        pl.semaphore_signal(barrier, inc=1, device_id=device, device_id_type=MESH)

    for d in range(1, NX):
        greet(at(xs(d), y, z, h))
        greet(at(xs(d), y, z, other))
    greet(at(x, y, z, other))
    for d in (1, 2, 6, 7):
        greet(at(x, ys(d), z, h))
    for d in range(1, NY):
        for child in range(2):
            greet(at(2 * child + half, ys(d), z, k))
    for d in (1, 2, 6, 7):
        greet(at(x, y, zs(d), h))

    @pl.when(y != z)
    def _():
        greet(at(x, z, y, h))

    loads[0].wait()
    for child in range(2):
        for tile in range(2):
            number = mask_ref[child, tile].astype(F32)
            masked[child, 256 * tile : 256 * tile + 256] *= number

    @pl.when(y != z)
    def _():
        pl.semaphore_wait(barrier, 30)

    @pl.when(y == z)
    def _():
        pl.semaphore_wait(barrier, 29)

    def x_rows(to_half, p):
        return pl.ds(pl.multiple_of(64 * h + 32 * to_half + 16 * p, 16), 16)

    def x_send(p):
        made = []
        for d in (1, 3, 2):
            to = xs(d)
            made.append(
                copy(
                    xt.at[lax.div(to, 2), :, x_rows(lax.rem(to, 2), p), :],
                    xr.at[x, p],
                    at(to, y, z, h),
                )
            )
            made[-1].start()
        xr[x, p] = xt[k, :, x_rows(half, p), :]
        return made

    def chunk_rows(s):
        dist = EVEN[s] + parity * (ODD[s] - EVEN[s])
        sub = lax.div(ys(dist), 2)
        return pl.ds(pl.multiple_of(128 * sub, 128), 128)

    def c_send(s):
        made = []
        for d in (1, 3, 2):
            to = xs(d)
            made.append(
                copy(
                    masked.at[lax.div(to, 2), chunk_rows(s), :],
                    cr.at[parity, s, x],
                    at(to, y, z, h),
                )
            )
            made[-1].start()
        cr[parity, s, x] = masked[k, chunk_rows(s), :]
        return made

    c_copies = [c_send(0)]
    loads[1].wait()
    for child in range(2):
        for s in range(8):
            xt[child, s] = xin[child, :, 128 * s : 128 * s + 128].T
    x_copies = [x_send(0), x_send(1)]
    for s in range(1, 4):
        c_copies.append(c_send(s))
    forwards = [copy(cr.at[parity, s], cr.at[parity, s], at(x, y, z, other)) for s in range(4)]

    loads[2].wait()
    mine = tr.at[h, x]
    t_near = [copy(mine, mine, at(xs(d), y, z, h)) for d in (1, 3)]
    t_cores = [copy(mine, mine, at(x, y, z, other))]
    for made in t_near + t_cores:
        made.start()

    z_copies = []
    for d in (1, 3, 2):
        to = xs(d)
        z_copies.append(sent(xt.at[lax.div(to, 2), z], xz.at[x], at(to, y, z, h)))
    xz[x] = xt[k, z]

    def convert(which, src):
        core = lax.rem(y + which, 2)
        rows = pl.ds(pl.multiple_of(256 * src, 256), 256)
        for i in range(2):
            n = which + 2 * i
            for side in range(2):
                far = lax.rem(8 - n, 8) if side else n
                dist = jnp.where(n == 0, 4 * side, far)
                lanes = pl.ds(pl.multiple_of(128 * lax.div(ys(dist), 2), 128), 128)
                high, low = split(tr[core, src, :, lanes])
                th[n, rows, 128 * side : 128 * side + 128] = high
                tl[n, rows, 128 * side : 128 * side + 128] = low

    def x_take(p):
        for made in x_copies[p]:
            made.wait_recv()
        for src in range(4):
            high, low = split(xr[src, p].reshape(128, 128))
            lanes = slice(128 * src, 128 * src + 128)
            xb[p, :128, lanes] = high
            xb[p, 128:, lanes] = low

    def push(s):
        for made in c_copies[s]:
            made.wait_recv()
        forwards[s].start()

    def take(which, s):
        if s:
            @pl.when(parity == which)
            def _():
                push(s)

        @pl.when(parity != which)
        def _():
            forwards[s].wait_recv()

        return split(jnp.concatenate([cr[which, s, src] for src in range(4)], axis=1))

    def partial(rows, p):
        high, low = rows
        both = dot_nt(xb[p], high)
        return both[:128] + both[128:] + dot_nt(xb[p, :128], low)

    def y_at(d):
        return at(x, ys(d), z, h)

    near = (1, 7)
    over = (2, 6)
    push(0)
    x_take(0)
    rows4 = take(0, 0)
    first = [[None, None], [None, None]]
    moving = [[None, None], [None, None]]

    def far_factor(p):
        pb[4, p] = partial(rows4, p)
        for way in range(2):
            rows = pl.ds(64 * way, 64)
            first[p][way] = sent(pb.at[4, p, rows], rb.at[way, 0, p, rows], y_at(over[way]))

    def third_factor(rows, way, p):
        pb[3 + 2 * way, p] = partial(rows, p)
        moving[p][way] = sent(pb.at[3 + 2 * way, p], rb.at[way, 1, p], y_at(near[way]))

    far_factor(0)
    rows3 = take(1, 0)
    third_factor(rows3, 0, 0)
    rows5 = take(1, 1)
    third_factor(rows5, 1, 0)
    x_take(1)
    far_factor(1)
    third_factor(rows3, 0, 1)
    third_factor(rows5, 1, 1)
    for step in (2, 3):
        taken = []
        for way in range(2):
            slot = ((0, 1 + way), (1, 2 + way))[step - 2]
            taken.append(take(*slot))
        for p in range(2):
            for way in range(2):
                pb[4 - step if way == 0 else 4 + step, p] = partial(taken[way], p)
            for way in range(2):
                index = 4 - step if way == 0 else 4 + step
                moving[p][way].wait_recv()
                pb[index, p] += rb[way, step - 1, p]
                if step == 2:
                    first[p][way].wait_recv()
                    half_rows = slice(64 * way, 64 * way + 64)
                    pb[index, p, half_rows] += rb[way, 0, p, half_rows]
                moving[p][way] = sent(pb.at[index, p], rb.at[way, step, p], y_at(near[way]))
    rows0 = take(0, 3)
    for p in range(2):
        pb[0, p] = partial(rows0, p)
    convert(parity, x)

    def ring_send(p, step):
        made = []
        for way in range(2):
            index = ys((8 - step) % 8) if way == 0 else ys(step)
            if step == 2:
                ref = fg.at[index, p, pl.ds(64 * way, 64)]
                made.append(sent(ref, ref, y_at(over[way])))
            ref = fg.at[index, p]
            made.append(sent(ref, ref, y_at(near[way])))
        return made

    flips, flip_sems = [], []
    for p in range(2):
        flip_sems.append(count[0])
        flips.append(copy(fg.at[y, p], fy.at[y, p], at(x, z, y, h), keep=False))
    relays = []

    def relay(d, p):
        i = count[0]
        count[0] += 1
        relays.append(
            pltpu.make_async_remote_copy(
                src_ref=fg.at[ys(d), p], dst_ref=fy.at[ys(d), p], send_sem=send_sem.at[i],
                recv_sem=recv_sem.at[flip_sems[p]], device_id=at(x, y, zs(d), h),
                device_id_type=MESH,
            )
        )

        @pl.when(y == z)
        def _():
            relays[-1].start()

    apart = lax.rem(z - y + 8, 8)
    far_apart = y != z
    for d in near + over:
        far_apart = jnp.logical_and(far_apart, apart != d)

    def flip_start(made):
        @pl.when(far_apart)
        def _():
            made.start()

    ring = [None, None]
    for p in range(2):
        for way in range(2):
            moving[p][way].wait_recv()
        fg[y, p] = pb[0, p] + rb[0, 3, p] + rb[1, 3, p]
        ring[p] = ring_send(p, 0)
        flip_start(flips[p])

    @pl.when(y == z)
    def _():
        fy[z] = fg[y]

    for made in z_copies:
        made.wait_recv()
    high, low = split(jnp.concatenate([xz[src] for src in range(4)], axis=1))
    for p in range(2):
        gram[p] = partial((high, low), p)

    t_far = []
    for i in range(2):
        t_near[i].wait_recv()
        src = xs(3 - 2 * i)
        ref = tr.at[h, src, pl.ds(128 * i, 128)]
        t_far.append(sent(ref, ref, at(xs(1 + 2 * i), y, z, h)))
        ref = tr.at[h, src]
        t_cores.append(sent(ref, ref, at(x, y, z, other)))
    for p in range(2):
        for made in ring[p]:
            made.wait_recv()
        ring[p] = ring_send(p, 1)
        for d in near:
            relay(d, p)
    t_cores[0].wait_recv()
    convert(1 - parity, x)
    for i in range(2):
        convert(parity, xs(3 - 2 * i))
    for p in range(2):
        for made in ring[p]:
            made.wait_recv()
        ring[p] = ring_send(p, 2)
        for d in over:
            relay(d, p)

    def z_at(d):
        return at(x, y, zs(d), h)

    @pl.when(y != z)
    def _():
        for made in flips:
            made.wait_recv()

    def second_send(step):
        made = []
        for way in range(2):
            index = zs((8 - step) % 8) if way == 0 else zs(step)
            ref = fy.at[index, way] if step == 3 else fy.at[index]
            made.append(sent(ref, ref, z_at(near[way])))
        return made

    def second_next(step):
        for made in second[-1]:
            made.wait_recv()
        second.append(second_send(step))

    second = [second_send(0)]
    for i in range(2):
        t_cores[1 + i].wait_recv()
        convert(1 - parity, xs(3 - 2 * i))
    t_last = []
    for i in range(2):
        t_far[i].wait_recv()
        ref = tr.at[h, xs(2), pl.ds(128 * i, 128)]
        t_last.append(sent(ref, ref, at(x, y, z, other)))
    convert(parity, xs(2))
    for made in t_last:
        made.wait_recv()
    convert(1 - parity, xs(2))

    pairs = ((0, 4), (1, 7), (2, 6), (3, 5))

    def image_part(p):
        for made in ring[p]:
            made.wait_recv()
        highs, lows = [], []
        for a, b in pairs:
            high, low = split(jnp.concatenate([fg[ys(a), p], fg[ys(b), p]], axis=1))
            highs.append(jnp.concatenate([high, low], axis=0))
            lows.append(high)
        for n in range(4):
            lanes = slice(256 * n, 256 * n + 256)
            total = None
            for i in range(4):
                both = dot_nt(highs[i], th[i, lanes, :])
                part = both[:128] + both[128:] + dot_nt(lows[i], tl[i, lanes, :])
                total = part if total is None else total + part
            acc[p, :, :, lanes] = total.reshape(8, 16, 256)

    def image_first(p):
        for way in range(2):
            rows = pl.ds(8 * way, 8)
            first[p][way] = sent(acc.at[p, zs(4), rows], rd.at[p, way, 0, rows], z_at(over[way]))
            moving[p][way] = sent(acc.at[p, zs(3 + 2 * way)], rd.at[p, way, 1], z_at(near[way]))

    def image_step(p, step):
        for way in range(2):
            index = zs(4 - step) if way == 0 else zs(4 + step)
            moving[p][way].wait_recv()
            acc[p, index] += rd[p, way, step - 1]
            if step == 2:
                first[p][way].wait_recv()
                rows = pl.ds(8 * way, 8)
                acc[p, index, rows] += rd[p, way, 0, rows]
            moving[p][way] = sent(acc.at[p, index], rd.at[p, way, step], z_at(near[way]))

    image_part(0)
    image_first(0)
    image_part(1)
    image_first(1)
    for step in (2, 3):
        second_next(step - 1)
        for p in range(2):
            image_step(p, step)
    second_next(3)

    image_copies, image_cores, out_copies = [], [], []
    for p in range(2):
        for made in moving[p]:
            made.wait_recv()
        total = acc[p, z] + rd[p, 0, 3] + rd[p, 1, 3]
        img[own, p] = total
        neg[p] = -total
        pair = lax.rem(x + 1 - 2 * half + NX, NX)
        ref = img.at[own, p]
        image_copies.append(sent(ref, ref, at(pair, y, z, h)))
        image_cores.append(sent(ref, ref, at(x, y, z, other)))
    for p in range(2):
        for d in (1, 3, 2):
            to = xs(d)
            lanes = pl.ds(pl.multiple_of(256 * to, 256), 256)
            made = copy(neg.at[p, :, lanes], outr.at[x, p], at(to, y, z, h))
            made.start()
            out_copies.append(made)
        outr[x, p] = neg[p, :, pl.ds(pl.multiple_of(256 * x, 256), 256)]

    for p in range(2):
        image_copies[p].wait_recv()
        ref = img.at[2 * h + 1 - half, p]
        image_cores.append(sent(ref, ref, at(x, y, z, other)))
    for made in second[-1]:
        made.wait_recv()
    for c in range(8):
        block = 4 * (c % 2) + c // 2
        high, low = split(fy[c].reshape(256, 128))
        fyh[:, 128 * block : 128 * block + 128] = high
        fyl[:, 128 * block : 128 * block + 128] = low

    for made in image_cores:
        made.wait_recv()
    high, low = split(img[...].reshape(128, 1024))
    total = gram[...].reshape(256, 128) + dot3(fyh[...], fyl[...], high, low)
    total = total.reshape(2, 8, 16, 128)
    for ph in range(2):
        lanes = slice(64 * ph, 64 * ph + 64)
        ec[ph] = jnp.concatenate([total[0, :, :, lanes], total[1, :, :, lanes]], axis=-1)

    def last(d, ph, i):
        return pltpu.make_async_remote_copy(
            src_ref=ec.at[ph, ys(d)], dst_ref=er.at[k, d], send_sem=last_sem.at[16 + i],
            recv_sem=last_sem.at[8 * k + d], device_id=at(own, ys(d), z, ph), device_id_type=MESH,
        )

    order = (4, 3, 5, 2, 6, 1, 7, 0)
    for d in order:
        last(d, other, 8 + d).start()
        if d:
            last(d, h, d).start()

    @pl.when(h != k)
    def _():
        last(0, h, 0).start()

    @pl.when(h == k)
    def _():
        er[k, 0] = ec[h, y]

    for made in out_copies:
        made.wait_recv()
    for src in range(4):
        for p in range(2):
            start = 32 * (src % 2) + 16 * p
            cross_ref[src // 2, start : start + 16] = outr[src, p]

    def arrived(child, d):
        pltpu.make_async_remote_copy(
            src_ref=ec.at[0, 0], dst_ref=er.at[child, d], send_sem=last_sem.at[16],
            recv_sem=last_sem.at[8 * child + d], device_id=at(own, y, z, other),
            device_id_type=MESH,
        ).wait_recv()

    for child in range(2):
        for d in range(1, NY):
            arrived(child, d)

        @pl.when(jnp.logical_or(h != k, k != child))
        def _():
            arrived(child, 0)

        total = er[child, 0]
        for d in range(1, NY):
            total = total + er[child, d]
        child_ref[child, :16] = total[:, :64]
        child_ref[child, 16:] = total[:, 64:]

    for d in order:
        last(d, other, 8 + d).wait_send()
        if d:
            last(d, h, d).wait_send()

    @pl.when(h != k)
    def _():
        last(0, h, 0).wait_send()

    @pl.when(far_apart)
    def _():
        for made in flips:
            made.wait_send()

    @pl.when(y == z)
    def _():
        for made in relays:
            made.wait_send()

    for made in started:
        made.wait_send()


def local(top_inverse, coupling, child_inverse, tile_mask):
    vmem = pl.BlockSpec(memory_space=pltpu.VMEM)
    hbm = pl.BlockSpec(memory_space=pltpu.HBM)
    scratch = [
        pltpu.VMEM((2, 128, 1024), F32),
        pltpu.VMEM((2, 8, 128, 128), F32),
        pltpu.VMEM((2, 512, 128), F32),
        pltpu.VMEM((4, 2, 8, 16, 128), F32),
        pltpu.VMEM((4, 128, 128), F32),
        pltpu.VMEM((2, 4, 4, 128, 128), F32),
        pltpu.VMEM((2, 256, 512), BF16),
        pltpu.VMEM((2, 4, 256, 512), F32),
        pltpu.VMEM((4, 1024, 256), BF16),
        pltpu.VMEM((4, 1024, 256), BF16),
        pltpu.VMEM((8, 2, 128, 128), F32),
        pltpu.VMEM((2, 4, 2, 128, 128), F32),
        pltpu.VMEM((8, 2, 128, 128), F32),
        pltpu.VMEM((8, 2, 128, 128), F32),
        pltpu.VMEM((256, 1024), BF16),
        pltpu.VMEM((256, 1024), BF16),
        pltpu.VMEM((2, 8, 16, 1024), F32),
        pltpu.VMEM((2, 2, 4, 16, 1024), F32),
        pltpu.VMEM((4, 2, 16, 1024), F32),
        pltpu.VMEM((2, 16, 1024), F32),
        pltpu.VMEM((4, 2, 16, 256), F32),
        pltpu.VMEM((2, 8, 16, 128), F32),
        pltpu.VMEM((2, 8, 16, 128), F32),
        pltpu.VMEM((2, 128, 128), F32),
        pltpu.SemaphoreType.DMA((NSEM,)),
        pltpu.SemaphoreType.DMA((NSEM,)),
        pltpu.SemaphoreType.DMA((32,)),
        pltpu.SemaphoreType.DMA((3,)),
    ]
    cross, child = pl.pallas_call(
        kernel,
        out_shape=(
            jax.ShapeDtypeStruct((2, 64, 256), F32),
            jax.ShapeDtypeStruct((2, 32, 64), F32),
        ),
        in_specs=[hbm, hbm, hbm, pl.BlockSpec(memory_space=pltpu.SMEM)],
        out_specs=(vmem, vmem),
        scratch_shapes=scratch,
        compiler_params=pltpu.CompilerParams(
            collective_id=0, has_side_effects=True, vmem_limit_bytes=60 << 20
        ),
        name="selected_inverse",
    )(top_inverse, coupling, child_inverse, tile_mask)
    return jnp.transpose(cross, (1, 0, 2)), jnp.transpose(child, (1, 0, 2))


def solution(mesh):
    in_specs = (P("row", "col"), P(None, "col", "row"), P(None, "row", None), P(None, "col"))
    out_specs = (P("col", None, "row"), P("row", None, "col"))
    return jax.shard_map(local, mesh=mesh, in_specs=in_specs, out_specs=out_specs, check_vma=False)
```
